128 devices in a mesh: axial: 8 (over z, core), azim: 16 (over x, y).
Axes of the slice: x: 4, y: 4, z: 4, core: 2. Of those that a mesh axis runs over, the one named last changes fastest.
Arguments:
- fields: float32 [16384, 4, 1024], P(('axial', 'azim')), may hold values from -6 to 6
- new_owner: int32 [16384, 1], P(('axial', 'azim')), may hold values from 0 to 127; in each aligned block of 128 rows (0 to 127, 128 to 255, ...) at most 2 rows name the same one
- leaflet: bfloat16 [64, 256, 4096], P(None, 'axial', 'azim'), may hold values from -6 to 6
- stiffness: bfloat16 [64, 64], replicated, may hold values from -0.75 to 0.75
- coarse: float32 [8192, 256], P(('axial', 'azim')), may hold values from -6 to 6
- coarse_of_slot: int32 [32768], P(('axial', 'azim')), may hold values from 0 to 63
- viscosity: float32 [4], replicated, may hold values from 0.02 to 0.2
Outputs:
- regridded: float32 [32768, 4, 1024], P(('axial', 'azim'))
The draws below stay inside these ranges and needn't reach their ends.
Inputs may be any that keep to these rules, and one draw needn't show every extreme that they name: `new_owner`: among the patches of one device, at most 2 share a new owner; in some device's patches exactly 2 do.
All inputs are finite; a program needn't handle non-finite values.
Results may differ from the reference program's by a relative error of at most 0.004.
Values may be sent and summed in bfloat16 or wider, within the bound.
No kernel may reach another device: no remote copies, remote signals or barrier semaphores. Data moves between devices by JAX's collectives and lax.ppermute only.
A program may use at most 64 MiB of HBM per device.

```python
import math
import jax
import jax.numpy as jnp
import numpy as np
from jax import lax

PR = 16
PC = 64
FIELDS = 4
REC = 64
ZP = 4
CC = 64
STEPS = 2
P_DEV = 128
SC = 2
RS = 256
P_TOTAL = 16384
NA_DEV = 32
NZ_DEV = 256
N_AXIAL = 8
N_AZIM = 16
DEVICES = 128


def plant(values, own_key, low, high):
    extent = values.shape
    index_at = [jax.random.randint(jax.random.fold_in(own_key, axis), (), 0, extent[axis]) for axis in range(len(extent))]
    values = values.at[tuple(index_at)].set(low)
    longest = extent.index(max(extent))
    index_at[longest] = (index_at[longest] + 1) % extent[longest]
    return values.at[tuple(index_at)].set(high)


def block_levels(rng, dims, pieces, smallest, largest):
    def one(dim, parts):
        steps = jax.random.uniform(jax.random.fold_in(jax.random.fold_in(rng, 6), dim), (parts,), jnp.float32, smallest / len(pieces), largest / len(pieces))
        return jnp.repeat(jnp.exp(steps), dims[dim] // parts).reshape((-1,) + (1,) * (len(dims) - dim - 1))

    level = one(*pieces[0])
    for cut in pieces[1:]:
        level = level * one(*cut)
    return level


def routed_block(key, own, number, rows, count, top, most, lean):
    ranking = jax.random.permutation(key, count)
    heavy_load, common = shares(count, rows * top, most, lean, True), shares(count, rows * top, most, lean, False)
    places = jnp.arange(count)

    def named(sizes, turn):
        used = int((sizes > 0).sum())
        fixed = max(1, used // 4)
        passed = fixed + (places - fixed + turn * (used - fixed)) % max(1, count - fixed)
        return jnp.zeros((count,), jnp.int32).at[ranking[jnp.where(places < fixed, places, passed)]].set(jnp.asarray(sizes, jnp.int32))

    sizes = jnp.where(number % 4 == 0, named(heavy_load, number // 4), named(common, number - number // 4 - 1))
    mixed = jax.random.permutation(jax.random.fold_in(own, 3), count)
    giver, taker = mixed[0:count // 2 * 2:2], mixed[1:count // 2 * 2:2]
    margin = jnp.minimum(sizes[giver] - 1, most - sizes[taker]) // 2
    margin = jnp.where((giver == ranking[0]) | (taker == ranking[0]) | (sizes[taker] == 0), 0, jnp.maximum(margin, 0))
    passed = jax.random.randint(jax.random.fold_in(own, 4), (count // 2,), 0, 1 << 20) % (margin + 1)
    sizes = sizes.at[giver].add(-passed).at[taker].add(passed)
    items = jnp.searchsorted(jnp.cumsum(sizes), jnp.arange(rows * top), side="right").astype(jnp.int32)
    table = items.reshape(top, rows).T
    table = table[jax.random.permutation(jax.random.fold_in(own, 1), rows)]
    turn = jax.random.randint(jax.random.fold_in(own, 2), (rows, 1), 0, top)
    return jnp.take_along_axis(table, (jnp.arange(top)[None, :] + turn) % top, axis=1)


def shares(amount, total, most, lean, full):
    weights = [(1 << 20) // math.isqrt(standing ** lean) + 1 for standing in range(1, amount + 1)]
    largest = most if full else min(most, max(-(-total // amount), total * weights[0] // sum(weights)))
    least = 1 if total - largest >= amount - 1 else 0
    given, surplus = [largest] + [least] * (amount - 1), total - largest - least * (amount - 1)
    while surplus > 0:
        free = [i for i in range(1, amount) if given[i] < largest] or [i for i in range(1, amount) if given[i] < most]
        mass, budget = sum([weights[i] for i in free]), surplus
        for i in free:
            more = min(most - given[i], max(1, budget * weights[i] // mass), surplus)
            given[i] = given[i] + more
            surplus = surplus - more
    return np.array(given)


def noise(rng, shape, deviation, reach, cuts=(), kind=jnp.bfloat16):
    loudness = block_levels(rng, shape, cuts, -0.22, 0.18) if cuts else 1.0
    entries = jax.random.normal(rng, shape, jnp.float32) * deviation * loudness
    return jnp.minimum(jnp.maximum(entries, -reach), reach).astype(kind)


def setup_inputs(seed: int = 0) -> dict:
    arg_keys = jax.random.split(jax.random.key(seed), 8)
    fields = noise(arg_keys[0], (P_TOTAL, FIELDS, PR * PC), 1.0, 6.0, ((0, 128),), jnp.float32)
    new_owner_keys = jax.random.split(jax.random.fold_in(arg_keys[1], 1), P_TOTAL // P_DEV)
    new_owner_turns = jax.random.permutation(jax.random.fold_in(arg_keys[1], 3), P_TOTAL // P_DEV)
    new_owner = jax.vmap(lambda own, number: routed_block(jax.random.fold_in(arg_keys[1], 2), own, number, P_DEV, DEVICES, 1, SC, 2))(new_owner_keys, new_owner_turns).reshape((P_TOTAL, 1))
    leaflet = noise(arg_keys[2], (REC, NA_DEV * N_AXIAL, NZ_DEV * N_AZIM), 1.0, 6.0, ((1, 8), (2, 16)))
    stiffness = noise(arg_keys[3], (REC, REC), REC ** -0.5, 0.75)
    coarse = noise(arg_keys[4], (DEVICES * CC, FIELDS * PC), 1.0, 6.0, ((0, 128),), jnp.float32)
    coarse_of_slot = plant(jax.random.randint(arg_keys[5], (DEVICES * RS,), 0, CC), jax.random.fold_in(arg_keys[5], 1), 0, CC - 1).astype(jnp.int32)
    viscosity = jnp.clip(jax.random.uniform(arg_keys[6], (FIELDS,), jnp.float32, 0.02, 0.2), 0.02, 0.2)
    return dict(fields=fields, new_owner=new_owner, leaflet=leaflet, stiffness=stiffness, coarse=coarse, coarse_of_slot=coarse_of_slot, viscosity=viscosity)


SPREAD = 0.25


def interp_table(coarse_cols):
    fine_col = jnp.arange(2 * coarse_cols)
    nearest = fine_col // 2
    second = jnp.where(fine_col % 2 == 0, jnp.maximum(nearest - 1, 0), jnp.minimum(nearest + 1, coarse_cols - 1))
    coarse_row = jnp.arange(coarse_cols)[:, None]
    return 0.75 * (coarse_row == nearest[None, :]).astype(jnp.float32) + 0.25 * (coarse_row == second[None, :]).astype(jnp.float32)


def viscous(state, ghosts, viscosity):
    row_pad = jnp.concatenate([ghosts[:, :, 0:1, :], state, ghosts[:, :, 1:2, :]], axis=2)
    col_pad = jnp.pad(state, ((0, 0), (0, 0), (0, 0), (1, 1)))
    laplace = row_pad[:, :, 2:, :] + row_pad[:, :, :-2, :] + col_pad[:, :, :, 2:] + col_pad[:, :, :, :-2] - 4.0 * state
    return state + viscosity[None, :, None, None] * laplace


def reference(fields, new_owner, leaflet, stiffness, coarse, coarse_of_slot, viscosity):
    points = leaflet.astype(jnp.float32)
    padded = jnp.pad(points, ((0, 0), (1, 1), (0, 0)))
    laplace = padded[:, 2:, :] + padded[:, :-2, :] + jnp.roll(points, 1, 2) + jnp.roll(points, -1, 2) - 4.0 * points
    laplace = laplace.astype(jnp.bfloat16)
    tension = jnp.dot(stiffness, laplace.reshape(REC, -1), preferred_element_type=jnp.float32).astype(jnp.bfloat16)
    tension = tension.reshape(REC, N_AXIAL, NA_DEV, N_AZIM, ZP, PC)
    sheets = tension.transpose(1, 3, 2, 4, 0, 5).reshape(P_TOTAL, FIELDS, PR * PC)
    forced = fields + SPREAD * sheets.astype(jnp.float32)

    owners = new_owner.reshape(DEVICES, P_DEV)
    position = jnp.arange(P_DEV)

    def ranks(owner_row):
        earlier = (owner_row[:, None] == owner_row[None, :]) & (position[None, :] < position[:, None])
        return jnp.sum(earlier.astype(jnp.int32), axis=1)

    ranked = lax.map(ranks, owners)
    target = owners * RS + jnp.arange(DEVICES, dtype=jnp.int32)[:, None] * SC + ranked
    placed = jnp.zeros((DEVICES * RS, FIELDS, PR * PC), jnp.float32).at[target.reshape(-1).astype(jnp.int32)].set(forced)

    interp = interp_table(PC // 2)

    def relax(inputs):
        blocks, strips, picked = inputs
        chosen = jnp.take(strips, picked, axis=0).reshape(RS, FIELDS, 2, PC // 2)
        ghosts = jnp.einsum("sfgk,kc->sfgc", chosen, interp, precision=lax.Precision.HIGHEST)
        state = blocks.reshape(RS, FIELDS, PR, PC)
        for sweep in range(STEPS):
            state = viscous(state, ghosts, viscosity)
        return state.reshape(RS, FIELDS, PR * PC)

    result = lax.map(relax, (placed.reshape(DEVICES, RS, FIELDS, PR * PC), coarse.reshape(DEVICES, CC, FIELDS * PC), coarse_of_slot.reshape(DEVICES, RS)))
    return result.reshape(DEVICES * RS, FIELDS, PR * PC)
```

```python
import jax
import jax.numpy as jnp
import numpy as np
from jax import lax
from jax.experimental import pallas as pl
from jax.experimental.pallas import tpu as pltpu
from jax.sharding import PartitionSpec as P

PC = 64
FIELDS = 4
STEPS = 2
SPREAD = 0.25
LANES = 128
SUB = 8
SLOTS_EACH = 2
ALL = ("axial", "azim")


def to_tiles(x):
    n = x.shape[0]
    return x.reshape(n, FIELDS, -1, LANES).transpose(0, 2, 1, 3).reshape(n, -1, LANES)


def from_tiles(x):
    n = x.shape[0]
    return x.reshape(n, -1, FIELDS, LANES).transpose(0, 2, 1, 3).reshape(n, FIELDS, -1)


def halo(first, last, axis, wrap):
    size = lax.axis_size(axis)
    up = [(i, (i + 1) % size) for i in range(size if wrap else size - 1)]
    down = [(j, i) for i, j in up]
    return lax.ppermute(last, axis, up), lax.ppermute(first, axis, down)


def pack_kernel(target, fields, leaf, coupling, above, below, sides, out, lap, spread):
    block = pl.program_id(0)
    records, rows, cols = leaf.shape
    half = records // 2
    lane = lax.broadcasted_iota(jnp.int32, (half, LANES), 1)
    low = lane < PC

    @pl.when(block == 0)
    def _():
        def clear(i, _):
            out[pl.ds(i * 8, 8)] = jnp.zeros((8,) + out.shape[1:], out.dtype)
            return 0

        lax.fori_loop(0, out.shape[0] // 8, clear, 0)

        row_id = lax.broadcasted_iota(jnp.int32, (2, rows, cols), 1)
        col_id = lax.broadcasted_iota(jnp.int32, (2, rows, cols), 2)

        def one(i, _):
            x = leaf[pl.ds(2 * i, 2)].astype(jnp.float32)
            up = jnp.where(row_id == 0, 0.0, pltpu.roll(x, 1, 1))
            down = jnp.where(row_id == rows - 1, 0.0, pltpu.roll(x, rows - 1, 1))
            left = jnp.where(col_id == 0, 0.0, pltpu.roll(x, 1, 2))
            right = jnp.where(col_id == cols - 1, 0.0, pltpu.roll(x, cols - 1, 2))
            y = up + down + left + right - 4.0 * x
            for b in range(rows // SUB):
                part = y[:, b * SUB : (b + 1) * SUB].reshape(2 * SUB, cols)
                lap[b, pl.ds(pl.multiple_of(i * 2 * SUB, 2 * SUB), 2 * SUB)] = part.astype(lap.dtype)
            return 0

        lax.fori_loop(0, records // 2, one, 0)

        wide = records * SUB
        lift = (
            lax.broadcasted_iota(jnp.int32, (records, wide), 1) // SUB
            == lax.broadcasted_iota(jnp.int32, (records, wide), 0)
        ).astype(jnp.bfloat16)
        lifted = jnp.dot(coupling[...], lift, preferred_element_type=jnp.float32)
        within = lax.broadcasted_iota(jnp.int32, (half, wide), 1) % SUB
        for p in range(2):
            for r in range(SUB):
                part = jnp.where(within == r, lifted[p * half : (p + 1) * half], 0.0)
                at = (p * SUB + r) * half
                spread[at : at + half] = part.astype(spread.dtype)

    tension = jnp.dot(spread[...], lap[block], preferred_element_type=jnp.float32)
    edge = jnp.where(block == 0, above[...], jnp.zeros_like(above))
    edge_above = jnp.dot(coupling[...], edge, preferred_element_type=jnp.float32)
    edge = jnp.where(block == pl.num_programs(0) - 1, below[...], jnp.zeros_like(below))
    edge_below = jnp.dot(coupling[...], edge, preferred_element_type=jnp.float32)
    side = jnp.dot(coupling[...], sides[...], preferred_element_type=jnp.float32)
    quarters = cols // PC
    for r in range(SUB):
        row = block * SUB + r
        for t in range(cols // LANES):
            at = r * half
            a = tension[at : at + half, t * LANES : (t + 1) * LANES]
            at = (SUB + r) * half
            b = tension[at : at + half, t * LANES : (t + 1) * LANES]
            if r == 0:
                a = a + edge_above[:half, t * LANES : (t + 1) * LANES]
                b = b + edge_above[half:, t * LANES : (t + 1) * LANES]
            if r == SUB - 1:
                a = a + edge_below[:half, t * LANES : (t + 1) * LANES]
                b = b + edge_below[half:, t * LANES : (t + 1) * LANES]
            for h in range(2):
                q = 2 * t + h
                if h == 0:
                    sheet = jnp.where(low, a, pltpu.roll(b, PC, 1))
                else:
                    sheet = jnp.where(low, pltpu.roll(a, PC, 1), b)
                for which, cell in ((0, 0), (1, PC - 1)):
                    if q == which * (quarters - 1):
                        for p in range(2):
                            to = p * PC + cell
                            turn = lax.rem(to - which * rows - row + 2 * LANES, LANES)
                            moved = pltpu.roll(side[p * half : (p + 1) * half], turn, 1)
                            sheet = sheet + jnp.where(lane == to, moved, 0.0)
                n = quarters * r + q
                forced = fields[n] + sheet
                out[target[block * SUB * quarters + n]] = forced.astype(out.dtype)


def pack(target, fields, leaf, coupling, above, below, sides, slots):
    records, rows, cols = leaf.shape
    blocks = rows // SUB
    patches = fields.shape[0]
    whole = lambda *shape: pl.BlockSpec(shape, lambda b, *_: (0,) * len(shape))
    return pl.pallas_call(
        pack_kernel,
        grid_spec=pltpu.PrefetchScalarGridSpec(
            num_scalar_prefetch=1,
            grid=(blocks,),
            in_specs=[
                pl.BlockSpec((patches // blocks, records // 2, LANES), lambda b, *_: (b, 0, 0)),
                whole(records, rows, cols),
                whole(records, records),
                whole(records, cols),
                whole(records, cols),
                whole(records, LANES),
            ],
            out_specs=whole(slots, records // 2, LANES),
            scratch_shapes=[
                pltpu.VMEM((blocks, records * SUB, cols), jnp.bfloat16),
                pltpu.VMEM((records * SUB, records * SUB), jnp.bfloat16),
            ],
        ),
        out_shape=jax.ShapeDtypeStruct((slots, records // 2, LANES), jnp.bfloat16),
        compiler_params=pltpu.CompilerParams(vmem_limit_bytes=40 * 2**20),
    )(target, fields, leaf, coupling, above, below, sides)


def sweep_kernel(strip, state, ghosts, rate, out):
    block = pl.program_id(0)
    count = state.shape[0]
    lane = lax.broadcasted_iota(jnp.int32, (SUB, LANES), 1)
    row = lax.broadcasted_iota(jnp.int32, (SUB, LANES), 0)
    first = (lane < PC) & (row < FIELDS)
    last = (lane >= PC) & (row >= FIELDS)
    start = lane % PC == 0
    stop = lane % PC == PC - 1
    v = rate[...]
    keep = 1.0 - 4.0 * v
    tiles = state.shape[1] // SUB

    def one(s, _):
        g = ghosts[strip[block * count + s]]
        x = state[s].astype(jnp.float32)
        x = [x[k * SUB : (k + 1) * SUB] for k in range(tiles)]
        for _ in range(STEPS):
            across = [pltpu.roll(y, PC, 1) for y in x]
            ext = [g] + [pltpu.roll(y, FIELDS, 0) for y in across] + [g]
            new = []
            for k in range(tiles):
                vertical = across[k] + jnp.where(first, ext[k], jnp.where(last, ext[k + 2], ext[k + 1]))
                left = jnp.where(start, 0.0, pltpu.roll(x[k], 1, 1))
                right = jnp.where(stop, 0.0, pltpu.roll(x[k], LANES - 1, 1))
                new.append(keep * x[k] + v * (vertical + (left + right)))
            x = new
        for k in range(tiles):
            out[s, k * SUB : (k + 1) * SUB] = x[k]
        return 0

    lax.fori_loop(0, count, one, 0, unroll=4)


def sweeps(strip, state, ghosts, rate):
    slots, rows, _ = state.shape
    count = 32
    whole = lambda *shape: pl.BlockSpec(shape, lambda b, *_: (0,) * len(shape))
    return pl.pallas_call(
        sweep_kernel,
        grid_spec=pltpu.PrefetchScalarGridSpec(
            num_scalar_prefetch=1,
            grid=(slots // count,),
            in_specs=[
                pl.BlockSpec((count, rows, LANES), lambda b, *_: (b, 0, 0)),
                whole(*ghosts.shape),
                whole(SUB, LANES),
            ],
            out_specs=pl.BlockSpec((count, rows, LANES), lambda b, *_: (b, 0, 0)),
        ),
        out_shape=jax.ShapeDtypeStruct((slots, rows, LANES), jnp.float32),
        compiler_params=pltpu.CompilerParams(vmem_limit_bytes=40 * 2**20),
    )(strip, state, ghosts, rate)


def interp_table():
    coarse = PC // 2
    table = np.zeros((2, coarse, 2, PC), np.float32)
    for side in range(2):
        for c in range(PC):
            near = c // 2
            second = max(near - 1, 0) if c % 2 == 0 else min(near + 1, coarse - 1)
            table[side, near, side, c] += 0.75
            table[side, second, side, c] += 0.25
    return table.reshape(2 * coarse, 2 * PC)


def shards(fields, new_owner, leaflet, stiffness, coarse, coarse_of_slot, viscosity):
    devices = lax.axis_size("axial") * lax.axis_size("azim")
    patch_count = fields.shape[0]
    slots = devices * SLOTS_EACH
    records, rows, cols = leaflet.shape

    above, below = halo(leaflet[:, 0, :], leaflet[:, rows - 1, :], "axial", False)
    left, right = halo(leaflet[:, :, 0], leaflet[:, :, cols - 1], "azim", True)
    sides = jnp.concatenate([left, right, jnp.zeros((records, LANES - 2 * rows), leaflet.dtype)], axis=1)

    owners = new_owner[:, 0]
    position = jnp.arange(patch_count)
    earlier = (owners[:, None] == owners[None, :]) & (position[None, :] < position[:, None])
    ranked = jnp.sum(earlier.astype(jnp.int32), axis=1)
    target = owners * SLOTS_EACH + ranked

    coupling = (
        (stiffness * SPREAD).reshape(FIELDS, -1, 2, records).transpose(2, 1, 0, 3).reshape(records, records)
    )
    packed = pack(target, to_tiles(fields), leaflet, coupling, above, below, sides, slots)
    shaped = packed.reshape(devices, -1, LANES)
    arrived = lax.all_to_all(shaped, ALL, split_axis=0, concat_axis=0, tiled=True)
    state = arrived.reshape(slots, -1, LANES)

    strips = coarse.shape[0]
    ghosts = jnp.dot(
        coarse.reshape(strips * FIELDS, -1), jnp.asarray(interp_table()), precision=lax.Precision.HIGHEST
    ).reshape(strips, FIELDS, LANES)
    ghosts = jnp.concatenate([ghosts, ghosts], axis=1)
    rate = jnp.broadcast_to(jnp.concatenate([viscosity, viscosity])[:, None], (SUB, LANES))
    return from_tiles(sweeps(coarse_of_slot, state, ghosts, rate))


def solution(mesh):
    placed = (
        P(ALL, None, None),
        P(ALL, None),
        P(None, "axial", "azim"),
        P(),
        P(ALL, None),
        P(ALL),
        P(),
    )
    return jax.shard_map(
        shards,
        mesh=mesh,
        in_specs=placed,
        out_specs=P(ALL, None, None),
        check_vma=False,
    )
```

```python
import jax
import jax.numpy as jnp
import numpy as np
from jax import lax
from jax.experimental import pallas as pl
from jax.experimental.pallas import tpu as pltpu
from jax.sharding import PartitionSpec as P

PC = 64
FIELDS = 4
STEPS = 2
SPREAD = 0.25
LANES = 128
SUB = 8
SLOTS_EACH = 2
ALL = ("axial", "azim")
F32 = jnp.float32
BF16 = jnp.bfloat16
MIB = 2**20


def to_tiles(x):
    n = x.shape[0]
    return x.reshape(n, FIELDS, -1, LANES).transpose(0, 2, 1, 3).reshape(n, -1, LANES)


def from_tiles(x):
    n = x.shape[0]
    return x.reshape(n, -1, FIELDS, LANES).transpose(0, 2, 1, 3).reshape(n, FIELDS, -1)


def iota(shape, dim):
    return lax.broadcasted_iota(jnp.int32, shape, dim)


def dot(a, b):
    return jnp.dot(a, b, preferred_element_type=F32)


def where_one(mask):
    return jnp.where(mask, 1.0, 0.0).astype(BF16)


def edges_kernel(leaf, first, last, sides):
    records, rows, cols = leaf.shape
    half = rows // 2
    pick = iota((records, records * half), 1) - iota((records, records * half), 0) * half
    first[...] = dot(where_one(pick == 0), leaf[:, :half].reshape(-1, cols)).astype(BF16)
    last[...] = dot(where_one(pick == half - 1), leaf[:, half:].reshape(-1, cols)).astype(BF16)
    spot = jnp.where(iota((cols, LANES), 1) // rows % 2 == 0, 0, cols - 1)
    wide = dot(leaf[...].reshape(-1, cols), where_one(iota((cols, LANES), 0) == spot))
    r = iota((records * rows, LANES), 0) % rows
    wide = jnp.where(iota((records * rows, LANES), 1) % rows == r, wide, 0.0).astype(BF16)
    gather = iota((records, records * rows), 1) // rows == iota((records, records * rows), 0)
    sides[...] = dot(where_one(gather), wide).astype(BF16)


def edges(leaf):
    records, rows, cols = leaf.shape
    shapes = [(records, cols), (records, cols), (records, LANES)]
    return pl.pallas_call(
        edges_kernel,
        out_shape=[jax.ShapeDtypeStruct(s, BF16) for s in shapes],
        compiler_params=pltpu.CompilerParams(vmem_limit_bytes=16 * MIB),
        cost_estimate=pl.CostEstimate(flops=10**8, bytes_accessed=MIB, transcendentals=0),
    )(leaf)


def halves(a, b, low, t):
    a, b = a[:, t * LANES : (t + 1) * LANES], b[:, t * LANES : (t + 1) * LANES]
    return jnp.where(low, a, pltpu.roll(b, PC, 1)), jnp.where(low, pltpu.roll(a, PC, 1), b)


def edge_patches(rows, quarters):
    return [
        (r, q) for r in range(rows) for q in range(quarters) if r in (0, rows - 1) or q in (0, quarters - 1)
    ]


def main_kernel(
    target, fields_hbm, leaf_hbm, coupling, sent, rest, fields, leaf, lap, spread, stage, zero, sem, zero_sem, load_sem, leaf_sem
):
    records, rows, cols = leaf.shape
    blocks = rows // SUB
    size = fields.shape[0] // blocks
    leaf_load = pltpu.make_async_copy(leaf_hbm, leaf, leaf_sem)
    leaf_load.start()
    loads = [
        pltpu.make_async_copy(fields_hbm.at[pl.ds(n * size, size)], fields.at[pl.ds(n * size, size)], load_sem.at[n])
        for n in range(blocks)
    ]
    for c in loads:
        c.start()
    half = records // 2
    quarters = cols // PC
    low = iota((half, LANES), 1) < PC

    zero[...] = jnp.zeros_like(zero)
    size = zero.shape[0]
    clears = [
        pltpu.make_async_copy(zero, sent.at[pl.ds(i * size, size)], zero_sem) for i in range(sent.shape[0] // size)
    ]
    for c in clears:
        c.start()

    wide = records * SUB
    lift = where_one(iota((records, wide), 1) // SUB == iota((records, wide), 0))
    lifted = dot(coupling[...], lift)
    within = iota((half, wide), 1) % SUB
    for p in range(2):
        for r in range(SUB):
            part = jnp.where(within == r, lifted[p * half : (p + 1) * half], 0.0)
            at = (p * SUB + r) * half
            spread[at : at + half] = part.astype(BF16)

    leaf_load.wait()
    group = 256 // rows
    a, b = iota((group * rows, group * rows), 0), iota((group * rows, group * rows), 1)
    beside = where_one((jnp.abs(a - b) == 1) & (a // rows == b // rows))
    a, b = iota((cols, cols), 0), iota((cols, cols), 1)
    along = jnp.where(a == b, -4.0, jnp.where(jnp.abs(a - b) == 1, 1.0, 0.0)).astype(BF16)
    for g in range(records // group):
        x = leaf[g * group : (g + 1) * group].reshape(group * rows, cols)
        y = (dot(beside, x) + dot(x, along)).reshape(group, rows, cols)
        for n in range(rows // SUB):
            part = y[:, n * SUB : (n + 1) * SUB].reshape(group * SUB, cols)
            lap[n, g * group * SUB : (g + 1) * group * SUB] = part.astype(BF16)

    for c in clears:
        c.wait()

    edge = {rq: i for i, rq in enumerate(edge_patches(rows, quarters))}
    for n in range(rows // SUB):
        tension = dot(spread[...], lap[n])
        loads[n].wait()
        for k in range(SUB):
            r = n * SUB + k
            a = tension[k * half : (k + 1) * half]
            b = tension[(SUB + k) * half : (SUB + k + 1) * half]
            for t in range(cols // LANES):
                for h, sheet in enumerate(halves(a, b, low, t)):
                    q = 2 * t + h
                    patch = r * quarters + q
                    forced = fields[patch] + sheet
                    if (r, q) in edge:
                        rest[edge[r, q]] = forced
                    else:
                        stage[patch] = forced.astype(BF16)
                        pltpu.make_async_copy(stage.at[patch], sent.at[target[patch]], sem).start()
    count = rows * quarters - len(edge)
    pltpu.make_async_copy(stage.at[pl.ds(0, count)], sent.at[pl.ds(0, count)], sem).wait()


def main_part(target, fields, leaf, coupling, slots):
    records, rows, cols = leaf.shape
    patches, tall, _ = fields.shape
    vmem = pl.BlockSpec(memory_space=pltpu.VMEM)
    hbm = pl.BlockSpec(memory_space=pltpu.HBM)
    count = len(edge_patches(rows, cols // PC))
    return pl.pallas_call(
        main_kernel,
        in_specs=[pl.BlockSpec(memory_space=pltpu.SMEM), hbm, hbm, vmem],
        out_specs=[hbm, vmem],
        out_shape=[
            pltpu.HBM((slots, tall, LANES), BF16),
            jax.ShapeDtypeStruct((count, tall, LANES), F32),
        ],
        scratch_shapes=[
            pltpu.VMEM(fields.shape, F32),
            pltpu.VMEM(leaf.shape, BF16),
            pltpu.VMEM((rows // SUB, records * SUB, cols), BF16),
            pltpu.VMEM((records * SUB, records * SUB), BF16),
            pltpu.VMEM((patches, tall, LANES), BF16),
            pltpu.VMEM((32, tall, LANES), BF16),
            pltpu.SemaphoreType.DMA,
            pltpu.SemaphoreType.DMA,
            pltpu.SemaphoreType.DMA((rows // SUB,)),
            pltpu.SemaphoreType.DMA,
        ],
        compiler_params=pltpu.CompilerParams(vmem_limit_bytes=24 * MIB),
        cost_estimate=pl.CostEstimate(flops=2 * 10**9, bytes_accessed=8 * MIB, transcendentals=0),
    )(target, fields, leaf, coupling)


def edge_kernel(target, rest, coupling, above, below, left, right, sent_in, sent, stage, sem):
    del sent_in
    records, cols = above.shape
    half = records // 2
    quarters = cols // PC
    rows = LANES // 4
    low = iota((half, LANES), 1) < PC

    lane = iota((records, LANES), 1)
    near = jnp.where(lane // rows % 2 == 0, right[...].astype(F32), left[...].astype(F32)).astype(BF16)
    both = dot(coupling[...], near)
    both = jnp.where(low, both[:half], both[half:])
    lane = iota((half, LANES), 1)
    column = jnp.concatenate([jnp.where(lane % rows == r, both, 0.0) for r in range(rows)], axis=0)
    high = column.astype(BF16)
    split = jnp.concatenate([high, (column - high.astype(F32)).astype(BF16)], axis=1)
    a, b = iota((2 * LANES, 2 * LANES), 0), iota((2 * LANES, 2 * LANES), 1)
    p, s = a // PC % 2, a // rows % 2
    split = dot(split, where_one(b == jnp.where(s == 1, p * PC, LANES + p * PC + PC - 1)))

    ends = {}
    for r, row in ((0, above), (rows - 1, below)):
        whole = dot(coupling[...], row[...])
        for t in range(cols // LANES):
            for h, sheet in enumerate(halves(whole[:half], whole[half:], low, t)):
                ends[r, 2 * t + h] = sheet

    listed = edge_patches(rows, quarters)
    for i, (r, q) in enumerate(listed):
        forced = rest[i]
        if q == 0:
            forced = forced + split[r * half : (r + 1) * half, :LANES]
        if q == quarters - 1:
            forced = forced + split[r * half : (r + 1) * half, LANES:]
        if (r, q) in ends:
            forced = forced + ends[r, q]
        stage[i] = forced.astype(BF16)
        pltpu.make_async_copy(stage.at[i], sent.at[target[r * quarters + q]], sem).start()
    count = len(listed)
    pltpu.make_async_copy(stage, sent.at[pl.ds(0, count)], sem).wait()


def edge_part(target, rest, coupling, above, below, left, right, sent):
    vmem = pl.BlockSpec(memory_space=pltpu.VMEM)
    return pl.pallas_call(
        edge_kernel,
        in_specs=[pl.BlockSpec(memory_space=pltpu.SMEM)] + [vmem] * 6 + [pl.BlockSpec(memory_space=pltpu.HBM)],
        out_specs=pl.BlockSpec(memory_space=pltpu.HBM),
        out_shape=pltpu.HBM(sent.shape, sent.dtype),
        scratch_shapes=[pltpu.VMEM(rest.shape, BF16), pltpu.SemaphoreType.DMA],
        input_output_aliases={7: 0},
        compiler_params=pltpu.CompilerParams(vmem_limit_bytes=16 * MIB),
        cost_estimate=pl.CostEstimate(flops=2 * 10**8, bytes_accessed=2 * MIB, transcendentals=0),
    )(target, rest, coupling, above, below, left, right, sent)


def sweep_kernel(strip, state, ghosts, rate, shift, out):
    block = pl.program_id(0)
    count, tall, _ = state.shape
    lane = iota((SUB, LANES), 1)
    row = iota((SUB, LANES), 0)
    first = (lane < PC) & (row < FIELDS)
    last = (lane >= PC) & (row >= FIELDS)
    v = rate[...]
    tiles = tall // SUB
    chunk = 8

    def sweep(x, g, y):
        flat = [y[k * SUB : (k + 1) * SUB, :LANES] for k in range(tiles)]
        across = [y[k * SUB : (k + 1) * SUB, LANES:] for k in range(tiles)]
        ext = [g] + [pltpu.roll(z, FIELDS, 0) for z in across] + [g]
        new = []
        for k in range(tiles):
            vertical = jnp.where(first, ext[k], jnp.where(last, ext[k + 2], ext[k + 1]))
            new.append(x[k] + v * ((flat[k] + across[k]) + vertical))
        return new

    for c in range(count // chunk):
        slots = range(c * chunk, (c + 1) * chunk)
        x = state[c * chunk : (c + 1) * chunk].reshape(chunk * tall, LANES)
        y = dot(x, shift[:LANES])
        xs = []
        gs = []
        for i, s in enumerate(slots):
            gs.append(ghosts[strip[block * count + s]])
            mine = x[i * tall : (i + 1) * tall].astype(F32)
            mine = [mine[k * SUB : (k + 1) * SUB] for k in range(tiles)]
            xs.append(sweep(mine, gs[i], y[i * tall : (i + 1) * tall]))
        for step in range(STEPS - 1):
            flat = jnp.concatenate([z for mine in xs for z in mine], axis=0)
            high = flat.astype(BF16)
            y = dot(jnp.concatenate([high, (flat - high.astype(F32)).astype(BF16)], axis=1), shift[...])
            xs = [sweep(xs[i], gs[i], y[i * tall : (i + 1) * tall]) for i in range(chunk)]
        for i, s in enumerate(slots):
            for k in range(tiles):
                out[s, k * SUB : (k + 1) * SUB] = xs[i][k]


def shift_table():
    table = np.zeros((LANES, 2 * LANES), np.float32)
    for i in range(LANES):
        table[i, i] = -4.0
        for j in (i - 1, i + 1):
            if 0 <= j and j // PC == i // PC:
                table[i, j] = 1.0
        table[i, LANES + (i + PC) % LANES] = 1.0
    return np.concatenate([table, table], axis=0)


def sweeps(strip, state, ghosts, rate):
    slots, rows, _ = state.shape
    count = 32
    whole = lambda *shape: pl.BlockSpec(shape, lambda b, *_: (0,) * len(shape))
    return pl.pallas_call(
        sweep_kernel,
        grid_spec=pltpu.PrefetchScalarGridSpec(
            num_scalar_prefetch=1,
            grid=(slots // count,),
            in_specs=[
                pl.BlockSpec((count, rows, LANES), lambda b, *_: (b, 0, 0)),
                whole(*ghosts.shape),
                whole(SUB, LANES),
                whole(2 * LANES, 2 * LANES),
            ],
            out_specs=pl.BlockSpec((count, rows, LANES), lambda b, *_: (b, 0, 0)),
        ),
        out_shape=jax.ShapeDtypeStruct((slots, rows, LANES), F32),
        compiler_params=pltpu.CompilerParams(vmem_limit_bytes=24 * MIB),
    )(strip, state, ghosts, rate, jnp.asarray(shift_table(), BF16))


def interp_table():
    coarse = PC // 2
    table = np.zeros((2, coarse, 2, PC), np.float32)
    for side in range(2):
        for c in range(PC):
            near = c // 2
            second = max(near - 1, 0) if c % 2 == 0 else min(near + 1, coarse - 1)
            table[side, near, side, c] += 0.75
            table[side, second, side, c] += 0.25
    return table.reshape(2 * coarse, 2 * PC)


def shards(fields, new_owner, leaflet, stiffness, coarse, coarse_of_slot, viscosity):
    devices = lax.axis_size("axial") * lax.axis_size("azim")
    patch_count = fields.shape[0]
    slots = devices * SLOTS_EACH
    records = leaflet.shape[0]

    first, last, sides = edges(leaflet)
    size = lax.axis_size("axial")
    up = [(i, i + 1) for i in range(size - 1)]
    above = lax.ppermute(last, "axial", up)
    below = lax.ppermute(first, "axial", [(j, i) for i, j in up])
    size = lax.axis_size("azim")
    around = [(i, (i + 1) % size) for i in range(size)]
    left = lax.ppermute(sides, "azim", around)
    right = lax.ppermute(sides, "azim", [(j, i) for i, j in around])

    owners = new_owner[:, 0]
    position = jnp.arange(patch_count)
    earlier = (owners[:, None] == owners[None, :]) & (position[None, :] < position[:, None])
    ranked = jnp.sum(earlier.astype(jnp.int32), axis=1)
    target = owners * SLOTS_EACH + ranked

    coupling = (
        (stiffness * SPREAD).reshape(FIELDS, -1, 2, records).transpose(2, 1, 0, 3).reshape(records, records)
    )
    hbm = lambda x: pltpu.with_memory_space_constraint(x, pltpu.HBM)
    sent, rest = main_part(target, hbm(to_tiles(fields)), hbm(leaflet), coupling, slots)
    sent = edge_part(target, rest, coupling, above, below, left, right, sent)
    arrived = lax.all_to_all(sent.reshape(devices, -1, LANES), ALL, split_axis=0, concat_axis=0, tiled=True)
    state = arrived.reshape(slots, -1, LANES)

    strips = coarse.shape[0]
    ghosts = jnp.dot(
        coarse.reshape(strips * FIELDS, -1), jnp.asarray(interp_table()), precision=lax.Precision.HIGHEST
    ).reshape(strips, FIELDS, LANES)
    ghosts = jnp.concatenate([ghosts, ghosts], axis=1)
    rate = jnp.broadcast_to(jnp.concatenate([viscosity, viscosity])[:, None], (SUB, LANES))
    return from_tiles(sweeps(coarse_of_slot, state, ghosts, rate))


def solution(mesh):
    placed = (
        P(ALL, None, None),
        P(ALL, None),
        P(None, "axial", "azim"),
        P(),
        P(ALL, None),
        P(ALL),
        P(),
    )
    return jax.shard_map(
        shards,
        mesh=mesh,
        in_specs=placed,
        out_specs=P(ALL, None, None),
        check_vma=False,
    )
```

```python
import functools

import jax
import jax.numpy as jnp
import numpy as np
from jax import lax
from jax.experimental import pallas as pl
from jax.experimental.pallas import tpu as pltpu
from jax.sharding import PartitionSpec as P

PC = 64
FIELDS = 4
STEPS = 2
SPREAD = 0.25
LANES = 128
SUB = 8
SLOTS_EACH = 2
ALL = ("axial", "azim")
F32 = jnp.float32
BF16 = jnp.bfloat16
MIB = 2**20


def to_tiles(x):
    n = x.shape[0]
    return x.reshape(n, FIELDS, -1, LANES).transpose(0, 2, 1, 3).reshape(n, -1, LANES)


def from_tiles(x):
    n = x.shape[0]
    return x.reshape(n, -1, FIELDS, LANES).transpose(0, 2, 1, 3).reshape(n, FIELDS, -1)


def iota(shape, dim):
    return lax.broadcasted_iota(jnp.int32, shape, dim)


def dot(a, b):
    return jnp.dot(a, b, preferred_element_type=F32)


def in_hbm(x):
    return pltpu.with_memory_space_constraint(x, pltpu.HBM)


def where_one(mask):
    return jnp.where(mask, 1.0, 0.0).astype(BF16)


def edges_kernel(leaf_hbm, leaf, first, last, sides, sent, zero, load_sem, zero_sem):
    records, rows, cols = leaf.shape
    size = 16
    loads = []
    for n in range(records // size):
        part = pl.ds(n * size, size)
        loads.append(pltpu.make_async_copy(leaf_hbm.at[part], leaf.at[part], load_sem.at[n]))
        loads[n].start()
    zero[...] = jnp.zeros_like(zero)
    count = zero.shape[0]
    clears = [
        pltpu.make_async_copy(zero, sent.at[pl.ds(i * count, count)], zero_sem) for i in range(sent.shape[0] // count)
    ]
    for c in clears:
        c.start()

    a, b = iota((2 * size, size * rows), 0), iota((2 * size, size * rows), 1)
    ends = where_one(b == a % size * rows + a // size * (rows - 1))
    spot = jnp.where(iota((cols, LANES), 1) // rows % 2 == 0, 0, cols - 1)
    spot = where_one(iota((cols, LANES), 0) == spot)
    mine = iota((size * rows, LANES), 1) % rows == iota((size * rows, LANES), 0) % rows
    gather = where_one(iota((size, size * rows), 1) // rows == iota((size, size * rows), 0))
    for n in range(records // size):
        loads[n].wait()
        part = slice(n * size, (n + 1) * size)
        x = leaf[part].reshape(size * rows, cols)
        both = dot(ends, x).astype(BF16)
        first[part] = both[:size]
        last[part] = both[size:]
        sides[part] = dot(gather, jnp.where(mine, dot(x, spot), 0.0).astype(BF16)).astype(BF16)
    for c in clears:
        c.wait()


def edges(leaf, slots):
    records, rows, cols = leaf.shape
    vmem = pl.BlockSpec(memory_space=pltpu.VMEM)
    hbm = pl.BlockSpec(memory_space=pltpu.HBM)
    shapes = [leaf.shape, (records, cols), (records, cols), (records, LANES)]
    tile = (records // 2, LANES)
    return pl.pallas_call(
        edges_kernel,
        in_specs=[hbm],
        out_specs=[vmem] * 4 + [hbm],
        out_shape=[pltpu.VMEM(s, BF16) for s in shapes] + [pltpu.HBM((slots,) + tile, BF16)],
        scratch_shapes=[
            pltpu.VMEM((32,) + tile, BF16),
            pltpu.SemaphoreType.DMA((records // 16,)),
            pltpu.SemaphoreType.DMA,
        ],
        compiler_params=pltpu.CompilerParams(vmem_limit_bytes=16 * MIB),
        cost_estimate=pl.CostEstimate(flops=10**8, bytes_accessed=MIB, transcendentals=0),
    )(in_hbm(leaf))


def prepare_kernel(owner, stiffness, target, coupling, spread):
    devices, patches = LANES, owner.shape[1]
    mine = owner[...] == iota((devices, patches), 0)
    before = where_one(iota((patches, patches), 0) < iota((patches, patches), 1))
    earlier = dot(where_one(mine), before)
    ranked = jnp.sum(jnp.where(mine, earlier, 0.0), axis=0, keepdims=True)
    target[...] = owner[...] * SLOTS_EACH + ranked.astype(jnp.int32)

    records = stiffness.shape[0]
    half = records // 2
    a, b = iota((records, records), 0), iota((records, records), 1)
    old = a % FIELDS * (records // FIELDS) + a % half // FIELDS * 2 + a // half
    ordered = (dot(where_one(b == old), stiffness[...]) * SPREAD).astype(BF16)
    coupling[...] = ordered

    wide = records * SUB
    lift = where_one(iota((records, wide), 1) // SUB == iota((records, wide), 0))
    lifted = dot(ordered, lift)
    within = iota((half, wide), 1) % SUB
    for p in range(2):
        for r in range(SUB):
            part = jnp.where(within == r, lifted[p * half : (p + 1) * half], 0.0)
            at = (p * SUB + r) * half
            spread[at : at + half] = part.astype(BF16)


def prepare(owner, stiffness):
    vmem = pl.BlockSpec(memory_space=pltpu.VMEM)
    records = stiffness.shape[0]
    return pl.pallas_call(
        prepare_kernel,
        in_specs=[vmem] * 2,
        out_specs=[vmem] * 3,
        out_shape=[
            jax.ShapeDtypeStruct(owner.shape, jnp.int32),
            pltpu.VMEM((records, records), BF16),
            pltpu.VMEM((records * SUB, records * SUB), BF16),
        ],
        compiler_params=pltpu.CompilerParams(vmem_limit_bytes=16 * MIB),
        cost_estimate=pl.CostEstimate(flops=10**8, bytes_accessed=MIB, transcendentals=0),
    )(owner, stiffness)


def laplace_kernel(fields_hbm, leaf, fields, lap, sem):
    load = pltpu.make_async_copy(fields_hbm, fields, sem)
    load.start()
    records, rows, cols = leaf.shape
    group = 256 // rows
    a, b = iota((group * rows, group * rows), 0), iota((group * rows, group * rows), 1)
    beside = where_one((jnp.abs(a - b) == 1) & (a // rows == b // rows))
    a, b = iota((cols, cols), 0), iota((cols, cols), 1)
    along = jnp.where(a == b, -4.0, jnp.where(jnp.abs(a - b) == 1, 1.0, 0.0)).astype(BF16)
    for g in range(records // group):
        x = leaf[g * group : (g + 1) * group].reshape(group * rows, cols)
        y = (dot(beside, x) + dot(x, along)).reshape(group, rows, cols)
        for n in range(rows // SUB):
            part = y[:, n * SUB : (n + 1) * SUB].reshape(group * SUB, cols)
            lap[n, g * group * SUB : (g + 1) * group * SUB] = part.astype(BF16)
    load.wait()


def laplace(fields, leaf):
    records, rows, cols = leaf.shape
    vmem = pl.BlockSpec(memory_space=pltpu.VMEM)
    hbm = pl.BlockSpec(memory_space=pltpu.HBM)
    return pl.pallas_call(
        laplace_kernel,
        in_specs=[hbm, vmem],
        out_specs=[vmem] * 2,
        out_shape=[
            pltpu.VMEM(fields.shape, F32),
            pltpu.VMEM((rows // SUB, records * SUB, cols), BF16),
        ],
        scratch_shapes=[pltpu.SemaphoreType.DMA],
        compiler_params=pltpu.CompilerParams(vmem_limit_bytes=16 * MIB),
        cost_estimate=pl.CostEstimate(flops=5 * 10**8, bytes_accessed=3 * MIB, transcendentals=0),
    )(in_hbm(fields), leaf)


def halves(a, b, low, t):
    a, b = a[:, t * LANES : (t + 1) * LANES], b[:, t * LANES : (t + 1) * LANES]
    return jnp.where(low, a, pltpu.roll(b, PC, 1)), jnp.where(low, pltpu.roll(a, PC, 1), b)


def edge_patches(rows, quarters, span):
    ends = (0, rows - 1)
    return [
        (r, q) for r in range(rows) for q in range(quarters) if r // SUB in span and (r in ends or q in (0, quarters - 1))
    ]


def main_kernel(span, target, fields, lap, spread, sent_in, sent, rest, stage, sem):
    del sent_in
    blocks, _, cols = lap.shape
    half = fields.shape[1]
    rows = blocks * SUB
    quarters = cols // PC
    low = iota((half, LANES), 1) < PC
    listed = edge_patches(rows, quarters, span)
    edge = {rq: i for i, rq in enumerate(listed)}
    for n in span:
        tension = dot(spread[...], lap[n])
        for k in range(SUB):
            r = n * SUB + k
            a = tension[k * half : (k + 1) * half]
            b = tension[(SUB + k) * half : (SUB + k + 1) * half]
            for t in range(cols // LANES):
                for h, sheet in enumerate(halves(a, b, low, t)):
                    q = 2 * t + h
                    patch = r * quarters + q
                    forced = fields[patch] + sheet
                    if (r, q) in edge:
                        rest[edge[r, q]] = forced
                    else:
                        stage[patch] = forced.astype(BF16)
                        pltpu.make_async_copy(stage.at[patch], sent.at[target[0, patch]], sem).start()
    count = len(span) * SUB * quarters - len(edge)
    pltpu.make_async_copy(stage.at[pl.ds(0, count)], sent.at[pl.ds(0, count)], sem).wait()


def main_part(span, target, fields, lap, spread, sent):
    patches, tall, _ = fields.shape
    blocks, _, cols = lap.shape
    vmem = pl.BlockSpec(memory_space=pltpu.VMEM)
    hbm = pl.BlockSpec(memory_space=pltpu.HBM)
    count = len(edge_patches(blocks * SUB, cols // PC, span))
    return pl.pallas_call(
        functools.partial(main_kernel, span),
        in_specs=[pl.BlockSpec(memory_space=pltpu.SMEM), vmem, vmem, vmem, hbm],
        out_specs=[hbm, vmem],
        out_shape=[pltpu.HBM(sent.shape, BF16), pltpu.VMEM((count, tall, LANES), F32)],
        scratch_shapes=[pltpu.VMEM((patches, tall, LANES), BF16), pltpu.SemaphoreType.DMA],
        input_output_aliases={4: 0},
        compiler_params=pltpu.CompilerParams(vmem_limit_bytes=16 * MIB),
        cost_estimate=pl.CostEstimate(flops=10**9, bytes_accessed=4 * MIB, transcendentals=0),
    )(target, fields, lap, spread, sent)


def edge_kernel(target, rest_low, rest_high, coupling, above, below, left, right, sent_in, sent, stage, sem):
    del sent_in
    records, cols = above.shape
    half = records // 2
    quarters = cols // PC
    rows = LANES // 4
    low = iota((half, LANES), 1) < PC

    lane = iota((records, LANES), 1)
    near = jnp.where(lane // rows % 2 == 0, right[...].astype(F32), left[...].astype(F32)).astype(BF16)
    both = dot(coupling[...], near)
    both = jnp.where(low, both[:half], both[half:])
    lane = iota((half, LANES), 1)
    column = jnp.concatenate([jnp.where(lane % rows == r, both, 0.0) for r in range(rows)], axis=0)
    high = column.astype(BF16)
    split = jnp.concatenate([high, (column - high.astype(F32)).astype(BF16)], axis=1)
    a, b = iota((2 * LANES, 2 * LANES), 0), iota((2 * LANES, 2 * LANES), 1)
    p, s = a // PC % 2, a // rows % 2
    split = dot(split, where_one(b == jnp.where(s == 1, p * PC, LANES + p * PC + PC - 1)))

    ends = {}
    for r, row in ((0, above), (rows - 1, below)):
        whole = dot(coupling[...], row[...])
        for t in range(cols // LANES):
            for h, sheet in enumerate(halves(whole[:half], whole[half:], low, t)):
                ends[r, 2 * t + h] = sheet

    listed = edge_patches(rows, quarters, range(rows // SUB))
    for i, (r, q) in enumerate(listed):
        forced = rest_low[i] if i < rest_low.shape[0] else rest_high[i - rest_low.shape[0]]
        if q == 0:
            forced = forced + split[r * half : (r + 1) * half, :LANES]
        if q == quarters - 1:
            forced = forced + split[r * half : (r + 1) * half, LANES:]
        if (r, q) in ends:
            forced = forced + ends[r, q]
        stage[i] = forced.astype(BF16)
        pltpu.make_async_copy(stage.at[i], sent.at[target[0, r * quarters + q]], sem).start()
    count = len(listed)
    pltpu.make_async_copy(stage, sent.at[pl.ds(0, count)], sem).wait()


def edge_part(target, rest_low, rest_high, coupling, above, below, left, right, sent):
    vmem = pl.BlockSpec(memory_space=pltpu.VMEM)
    return pl.pallas_call(
        edge_kernel,
        in_specs=[pl.BlockSpec(memory_space=pltpu.SMEM)] + [vmem] * 7 + [pl.BlockSpec(memory_space=pltpu.HBM)],
        out_specs=pl.BlockSpec(memory_space=pltpu.HBM),
        out_shape=pltpu.HBM(sent.shape, sent.dtype),
        scratch_shapes=[
            pltpu.VMEM((rest_low.shape[0] + rest_high.shape[0],) + rest_low.shape[1:], BF16),
            pltpu.SemaphoreType.DMA,
        ],
        input_output_aliases={8: 0},
        compiler_params=pltpu.CompilerParams(vmem_limit_bytes=16 * MIB),
        cost_estimate=pl.CostEstimate(flops=2 * 10**8, bytes_accessed=2 * MIB, transcendentals=0),
    )(target, rest_low, rest_high, coupling, above, below, left, right, sent)


def sweep_kernel(strip, state, ghosts, rate, shift, out, done, sem):
    count, tall, _ = state.shape
    lane = iota((SUB, LANES), 1)
    row = iota((SUB, LANES), 0)
    first = (lane < PC) & (row < FIELDS)
    last = (lane >= PC) & (row >= FIELDS)
    v = rate[...]
    tiles = tall // SUB
    chunk = 8

    def sweep(x, g, y):
        flat = [y[k * SUB : (k + 1) * SUB, :LANES] for k in range(tiles)]
        across = [y[k * SUB : (k + 1) * SUB, LANES:] for k in range(tiles)]
        ext = [g] + [pltpu.roll(z, FIELDS, 0) for z in across] + [g]
        new = []
        for k in range(tiles):
            vertical = jnp.where(first, ext[k], jnp.where(last, ext[k + 2], ext[k + 1]))
            new.append(x[k] + v * ((flat[k] + across[k]) + vertical))
        return new

    def one(c, _):
        base = pl.multiple_of(c * chunk, chunk)
        x = state[pl.ds(base, chunk)].reshape(chunk * tall, LANES)
        y = dot(x, shift[:LANES])
        xs = []
        gs = []
        for i in range(chunk):
            gs.append(ghosts[strip[base + i]])
            mine = x[i * tall : (i + 1) * tall].astype(F32)
            mine = [mine[k * SUB : (k + 1) * SUB] for k in range(tiles)]
            xs.append(sweep(mine, gs[i], y[i * tall : (i + 1) * tall]))
        for step in range(STEPS - 1):
            flat = jnp.concatenate([z for mine in xs for z in mine], axis=0)
            high = flat.astype(BF16)
            y = dot(jnp.concatenate([high, (flat - high.astype(F32)).astype(BF16)], axis=1), shift[...])
            xs = [sweep(xs[i], gs[i], y[i * tall : (i + 1) * tall]) for i in range(chunk)]
        for i in range(chunk):
            for k in range(tiles):
                done[base + i, k * SUB : (k + 1) * SUB] = xs[i][k]
        pltpu.make_async_copy(done.at[pl.ds(base, chunk)], out.at[pl.ds(base, chunk)], sem).start()
        return 0

    lax.fori_loop(0, count // chunk, one, 0, unroll=count // chunk)
    pltpu.make_async_copy(done, out, sem).wait()


def shift_table():
    table = np.zeros((LANES, 2 * LANES), np.float32)
    for i in range(LANES):
        table[i, i] = -4.0
        for j in (i - 1, i + 1):
            if 0 <= j and j // PC == i // PC:
                table[i, j] = 1.0
        table[i, LANES + (i + PC) % LANES] = 1.0
    return np.concatenate([table, table], axis=0)


def sweeps(strip, state, ghosts, rate):
    vmem = pl.BlockSpec(memory_space=pltpu.VMEM)
    return pl.pallas_call(
        sweep_kernel,
        in_specs=[pl.BlockSpec(memory_space=pltpu.SMEM)] + [vmem] * 4,
        out_specs=pl.BlockSpec(memory_space=pltpu.HBM),
        out_shape=pltpu.HBM(state.shape, F32),
        scratch_shapes=[pltpu.VMEM(state.shape, F32), pltpu.SemaphoreType.DMA],
        compiler_params=pltpu.CompilerParams(vmem_limit_bytes=24 * MIB),
    )(strip, state, ghosts, rate, jnp.asarray(shift_table(), BF16))


def interp_table():
    coarse = PC // 2
    table = np.zeros((2, coarse, 2, PC), np.float32)
    for side in range(2):
        for c in range(PC):
            near = c // 2
            second = max(near - 1, 0) if c % 2 == 0 else min(near + 1, coarse - 1)
            table[side, near, side, c] += 0.75
            table[side, second, side, c] += 0.25
    return table.reshape(2 * coarse, 2 * PC)


def shards(fields, new_owner, leaflet, stiffness, coarse, coarse_of_slot, viscosity):
    devices = lax.axis_size("axial") * lax.axis_size("azim")
    patch_count = fields.shape[0]
    slots = devices * SLOTS_EACH

    leaf, first, last, sides, sent = edges(leaflet, slots)
    size = lax.axis_size("azim")
    around = [(i, (i + 1) % size) for i in range(size)]
    right = lax.ppermute(sides, "azim", [(j, i) for i, j in around])
    target, coupling, spread = prepare(new_owner.reshape(1, patch_count), stiffness)
    sides, right, spread, leaf = lax.optimization_barrier((sides, right, spread, leaf))
    left = lax.ppermute(sides, "azim", around)
    held, lap = laplace(to_tiles(fields), leaf)
    first, last, left, lap = lax.optimization_barrier((first, last, left, lap))
    size = lax.axis_size("axial")
    up = [(i, i + 1) for i in range(size - 1)]
    above = lax.ppermute(last, "axial", up)
    blocks = lap.shape[0]
    sent, rest_low = main_part(range(blocks // 2), target, held, lap, spread, sent)
    first, above, sent = lax.optimization_barrier((first, above, sent))
    below = lax.ppermute(first, "axial", [(j, i) for i, j in up])
    sent, rest_high = main_part(range(blocks // 2, blocks), target, held, lap, spread, sent)
    sent = edge_part(target, rest_low, rest_high, coupling, above, below, left, right, sent)
    arrived = lax.all_to_all(sent.reshape(devices, -1, LANES), ALL, split_axis=0, concat_axis=0, tiled=True)
    state = arrived.reshape(slots, -1, LANES)

    strips = coarse.shape[0]
    ghosts = jnp.dot(
        coarse.reshape(strips * FIELDS, -1), jnp.asarray(interp_table()), precision=lax.Precision.HIGHEST
    ).reshape(strips, FIELDS, LANES)
    ghosts = jnp.concatenate([ghosts, ghosts], axis=1)
    rate = jnp.broadcast_to(jnp.concatenate([viscosity, viscosity])[:, None], (SUB, LANES))
    return from_tiles(sweeps(coarse_of_slot, state, ghosts, rate))


def solution(mesh):
    placed = (
        P(ALL, None, None),
        P(ALL, None),
        P(None, "axial", "azim"),
        P(),
        P(ALL, None),
        P(ALL),
        P(),
    )
    return jax.shard_map(
        shards,
        mesh=mesh,
        in_specs=placed,
        out_specs=P(ALL, None, None),
        check_vma=False,
    )
```

```python
import jax
import jax.numpy as jnp
import numpy as np
from jax import lax
from jax.experimental import pallas as pl
from jax.experimental.pallas import tpu as pltpu
from jax.sharding import PartitionSpec as P

PC = 64
FIELDS = 4
STEPS = 2
SPREAD = 0.25
LANES = 128
SUB = 8
SLOTS_EACH = 2
ALL = ("axial", "azim")
F32 = jnp.float32
BF16 = jnp.bfloat16
MIB = 2**20


def to_tiles(x):
    n = x.shape[0]
    return x.reshape(n, FIELDS, -1, LANES).transpose(0, 2, 1, 3).reshape(n, -1, LANES)


def from_tiles(x):
    n = x.shape[0]
    return x.reshape(n, -1, FIELDS, LANES).transpose(0, 2, 1, 3).reshape(n, FIELDS, -1)


def iota(shape, dim):
    return lax.broadcasted_iota(jnp.int32, shape, dim)


def dot(a, b):
    return jnp.dot(a, b, preferred_element_type=F32)


def in_hbm(x):
    return pltpu.with_memory_space_constraint(x, pltpu.HBM)


def where_one(mask):
    return jnp.where(mask, 1.0, 0.0).astype(BF16)


def first_kernel(
    leaf_hbm, owner_hbm, stiff_hbm, leaf, one, two, sides, target, coupling, spread, owner, stiffness, load_sem, small_sem
):
    records, rows, cols = leaf.shape
    small = [
        pltpu.make_async_copy(owner_hbm, owner, small_sem.at[0]),
        pltpu.make_async_copy(stiff_hbm, stiffness, small_sem.at[1]),
    ]
    for c in small:
        c.start()
    size = 16
    loads = []
    for n in range(records // size):
        part = pl.ds(n * size, size)
        loads.append(pltpu.make_async_copy(leaf_hbm.at[part], leaf.at[part], load_sem.at[n]))
        loads[n].start()

    small[0].wait()
    devices, patches = LANES, owner.shape[1]
    mine = owner[...] == iota((devices, patches), 0)
    before = where_one(iota((patches, patches), 0) < iota((patches, patches), 1))
    earlier = dot(where_one(mine), before)
    ranked = jnp.sum(jnp.where(mine, earlier, 0.0), axis=0, keepdims=True)
    target[...] = owner[...] * SLOTS_EACH + ranked.astype(jnp.int32)

    small[1].wait()
    half = records // 2
    a, b = iota((records, records), 0), iota((records, records), 1)
    old = a % FIELDS * (records // FIELDS) + a % half // FIELDS * 2 + a // half
    ordered = (dot(where_one(b == old), stiffness[...]) * SPREAD).astype(BF16)
    coupling[...] = ordered

    wide = records * SUB
    lift = where_one(iota((records, wide), 1) // SUB == iota((records, wide), 0))
    lifted = dot(ordered, lift)
    within = iota((half, wide), 1) % SUB
    for p in range(2):
        for r in range(SUB):
            part = jnp.where(within == r, lifted[p * half : (p + 1) * half], 0.0)
            at = (p * SUB + r) * half
            spread[at : at + half] = part.astype(BF16)

    odd = lax.axis_index("axial") % 2
    a, b = iota((2 * size, size * rows), 0), iota((2 * size, size * rows), 1)
    pick = jnp.where((a // size + odd) % 2 == 0, rows - 1, 0)
    ends = where_one(b == a % size * rows + pick)
    spot = jnp.where(iota((cols, LANES), 1) // rows % 2 == 0, 0, cols - 1)
    spot = where_one(iota((cols, LANES), 0) == spot)
    mine = iota((size * rows, LANES), 1) % rows == iota((size * rows, LANES), 0) % rows
    gather = where_one(iota((size, size * rows), 1) // rows == iota((size, size * rows), 0))
    for n in range(records // size):
        loads[n].wait()
        part = slice(n * size, (n + 1) * size)
        x = leaf[part].reshape(size * rows, cols)
        both = dot(ends, x).astype(BF16)
        one[part] = both[:size]
        two[part] = both[size:]
        sides[part] = dot(gather, jnp.where(mine, dot(x, spot), 0.0).astype(BF16)).astype(BF16)


def first_part(leaf, owner, stiffness):
    records, rows, cols = leaf.shape
    vmem = pl.BlockSpec(memory_space=pltpu.VMEM)
    hbm = pl.BlockSpec(memory_space=pltpu.HBM)
    shapes = [leaf.shape, (records, cols), (records, cols), (records, LANES)]
    return pl.pallas_call(
        first_kernel,
        in_specs=[hbm] * 3,
        out_specs=[vmem] * 7,
        out_shape=[pltpu.VMEM(s, BF16) for s in shapes]
        + [
            jax.ShapeDtypeStruct(owner.shape, jnp.int32),
            pltpu.VMEM((records, records), BF16),
            pltpu.VMEM((records * SUB, records * SUB), BF16),
        ],
        scratch_shapes=[
            pltpu.VMEM(owner.shape, jnp.int32),
            pltpu.VMEM(stiffness.shape, BF16),
            pltpu.SemaphoreType.DMA((records // 16,)),
            pltpu.SemaphoreType.DMA((2,)),
        ],
        compiler_params=pltpu.CompilerParams(vmem_limit_bytes=16 * MIB),
        cost_estimate=pl.CostEstimate(flops=10**8, bytes_accessed=MIB, transcendentals=0),
    )(in_hbm(leaf), in_hbm(owner), in_hbm(stiffness))


def laplace_kernel(fields_hbm, leaf, fields, lap, sent, zero, sem, zero_sem):
    load = pltpu.make_async_copy(fields_hbm, fields, sem)
    load.start()
    zero[...] = jnp.zeros_like(zero)
    count = zero.shape[0]
    clears = [
        pltpu.make_async_copy(zero, sent.at[pl.ds(i * count, count)], zero_sem) for i in range(sent.shape[0] // count)
    ]
    for c in clears:
        c.start()
    records, rows, cols = leaf.shape
    group = 256 // rows
    a, b = iota((group * rows, group * rows), 0), iota((group * rows, group * rows), 1)
    beside = where_one((jnp.abs(a - b) == 1) & (a // rows == b // rows))
    a, b = iota((cols, cols), 0), iota((cols, cols), 1)
    along = jnp.where(a == b, -4.0, jnp.where(jnp.abs(a - b) == 1, 1.0, 0.0)).astype(BF16)
    for g in range(records // group):
        x = leaf[g * group : (g + 1) * group].reshape(group * rows, cols)
        y = (dot(beside, x) + dot(x, along)).reshape(group, rows, cols)
        for n in range(rows // SUB):
            part = y[:, n * SUB : (n + 1) * SUB].reshape(group * SUB, cols)
            lap[n, g * group * SUB : (g + 1) * group * SUB] = part.astype(BF16)
    for c in clears:
        c.wait()
    load.wait()


def laplace(fields, leaf, slots):
    records, rows, cols = leaf.shape
    vmem = pl.BlockSpec(memory_space=pltpu.VMEM)
    hbm = pl.BlockSpec(memory_space=pltpu.HBM)
    return pl.pallas_call(
        laplace_kernel,
        in_specs=[hbm, vmem],
        out_specs=[vmem, vmem, hbm],
        out_shape=[
            pltpu.VMEM(fields.shape, F32),
            pltpu.VMEM((rows // SUB, records * SUB, cols), BF16),
            pltpu.HBM((slots,) + fields.shape[1:], BF16),
        ],
        scratch_shapes=[
            pltpu.VMEM((32,) + fields.shape[1:], BF16),
            pltpu.SemaphoreType.DMA,
            pltpu.SemaphoreType.DMA,
        ],
        compiler_params=pltpu.CompilerParams(vmem_limit_bytes=16 * MIB),
        cost_estimate=pl.CostEstimate(flops=5 * 10**8, bytes_accessed=3 * MIB, transcendentals=0),
    )(in_hbm(fields), leaf)


def exchange(x, axis, offset):
    size = lax.axis_size(axis)
    pairs = [(i % size, (i + 1) % size) for i in range(offset, size + offset, 2)]
    return lax.ppermute(x, axis, pairs + [(j, i) for i, j in pairs])


def halves(a, b, low, t):
    a, b = a[:, t * LANES : (t + 1) * LANES], b[:, t * LANES : (t + 1) * LANES]
    return jnp.where(low, a, pltpu.roll(b, PC, 1)), jnp.where(low, pltpu.roll(a, PC, 1), b)


def edge_patches(rows, quarters):
    return [
        (r, q) for r in range(rows) for q in range(quarters) if r in (0, rows - 1) or q in (0, quarters - 1)
    ]


def main_kernel(target, fields, lap, spread, sent_in, sent, rest, stage, sem):
    del sent_in
    blocks, _, cols = lap.shape
    half = fields.shape[1]
    rows = blocks * SUB
    quarters = cols // PC
    low = iota((half, LANES), 1) < PC
    listed = edge_patches(rows, quarters)
    edge = {rq: i for i, rq in enumerate(listed)}
    for n in range(blocks):
        tension = dot(spread[...], lap[n])
        for k in range(SUB):
            r = n * SUB + k
            a = tension[k * half : (k + 1) * half]
            b = tension[(SUB + k) * half : (SUB + k + 1) * half]
            for t in range(cols // LANES):
                for h, sheet in enumerate(halves(a, b, low, t)):
                    q = 2 * t + h
                    patch = r * quarters + q
                    forced = fields[patch] + sheet
                    if (r, q) in edge:
                        rest[edge[r, q]] = forced
                    else:
                        stage[patch] = forced.astype(BF16)
                        pltpu.make_async_copy(stage.at[patch], sent.at[target[0, patch]], sem).start()
    count = rows * quarters - len(edge)
    pltpu.make_async_copy(stage.at[pl.ds(0, count)], sent.at[pl.ds(0, count)], sem).wait()


def main_part(target, fields, lap, spread, sent):
    patches, tall, _ = fields.shape
    blocks, _, cols = lap.shape
    vmem = pl.BlockSpec(memory_space=pltpu.VMEM)
    hbm = pl.BlockSpec(memory_space=pltpu.HBM)
    count = len(edge_patches(blocks * SUB, cols // PC))
    return pl.pallas_call(
        main_kernel,
        in_specs=[pl.BlockSpec(memory_space=pltpu.SMEM), vmem, vmem, vmem, hbm],
        out_specs=[hbm, vmem],
        out_shape=[pltpu.HBM(sent.shape, BF16), pltpu.VMEM((count, tall, LANES), F32)],
        scratch_shapes=[pltpu.VMEM((patches, tall, LANES), BF16), pltpu.SemaphoreType.DMA],
        input_output_aliases={4: 0},
        compiler_params=pltpu.CompilerParams(vmem_limit_bytes=16 * MIB),
        cost_estimate=pl.CostEstimate(flops=10**9, bytes_accessed=4 * MIB, transcendentals=0),
    )(target, fields, lap, spread, sent)


def edge_kernel(target, rest, coupling, row_one, row_two, side_one, side_two, sent_in, sent, stage, sem):
    del sent_in
    records, cols = row_one.shape
    half = records // 2
    quarters = cols // PC
    rows = LANES // 4
    low = iota((half, LANES), 1) < PC

    lane = iota((records, LANES), 1)
    odd = lax.axis_index("azim") % 2
    near = jnp.where((lane // rows + odd) % 2 == 0, side_one[...].astype(F32), side_two[...].astype(F32)).astype(BF16)
    both = dot(coupling[...], near)
    both = jnp.where(low, both[:half], both[half:])
    lane = iota((half, LANES), 1)
    column = jnp.concatenate([jnp.where(lane % rows == r, both, 0.0) for r in range(rows)], axis=0)
    high = column.astype(BF16)
    split = jnp.concatenate([high, (column - high.astype(F32)).astype(BF16)], axis=1)
    a, b = iota((2 * LANES, 2 * LANES), 0), iota((2 * LANES, 2 * LANES), 1)
    p, s = a // PC % 2, a // rows % 2
    split = dot(split, where_one(b == jnp.where(s == 1, p * PC, LANES + p * PC + PC - 1)))

    place, size = lax.axis_index("axial"), lax.axis_size("axial")
    odd = place % 2 == 1
    one, two = row_one[...].astype(F32), row_two[...].astype(F32)
    two = jnp.where((place == 0) | (place == size - 1), 0.0, two)
    ends = {}
    for r, row in ((0, jnp.where(odd, one, two)), (rows - 1, jnp.where(odd, two, one))):
        whole = dot(coupling[...], row.astype(BF16))
        for t in range(cols // LANES):
            for h, sheet in enumerate(halves(whole[:half], whole[half:], low, t)):
                ends[r, 2 * t + h] = sheet

    listed = edge_patches(rows, quarters)
    for i, (r, q) in enumerate(listed):
        forced = rest[i]
        if q == 0:
            forced = forced + split[r * half : (r + 1) * half, :LANES]
        if q == quarters - 1:
            forced = forced + split[r * half : (r + 1) * half, LANES:]
        if (r, q) in ends:
            forced = forced + ends[r, q]
        stage[i] = forced.astype(BF16)
        pltpu.make_async_copy(stage.at[i], sent.at[target[0, r * quarters + q]], sem).start()
    count = len(listed)
    pltpu.make_async_copy(stage, sent.at[pl.ds(0, count)], sem).wait()


def edge_part(target, rest, coupling, row_one, row_two, side_one, side_two, sent):
    vmem = pl.BlockSpec(memory_space=pltpu.VMEM)
    return pl.pallas_call(
        edge_kernel,
        in_specs=[pl.BlockSpec(memory_space=pltpu.SMEM)] + [vmem] * 6 + [pl.BlockSpec(memory_space=pltpu.HBM)],
        out_specs=pl.BlockSpec(memory_space=pltpu.HBM),
        out_shape=pltpu.HBM(sent.shape, sent.dtype),
        scratch_shapes=[pltpu.VMEM(rest.shape, BF16), pltpu.SemaphoreType.DMA],
        input_output_aliases={7: 0},
        compiler_params=pltpu.CompilerParams(vmem_limit_bytes=16 * MIB),
        cost_estimate=pl.CostEstimate(flops=2 * 10**8, bytes_accessed=2 * MIB, transcendentals=0),
    )(target, rest, coupling, row_one, row_two, side_one, side_two, sent)


def sweep_kernel(strip, state, ghosts, rate, shift, out, done, sem):
    count, tall, _ = state.shape
    lane = iota((SUB, LANES), 1)
    row = iota((SUB, LANES), 0)
    first = (lane < PC) & (row < FIELDS)
    last = (lane >= PC) & (row >= FIELDS)
    v = rate[...]
    tiles = tall // SUB
    chunk = 8

    def sweep(x, g, y):
        flat = [y[k * SUB : (k + 1) * SUB, :LANES] for k in range(tiles)]
        across = [y[k * SUB : (k + 1) * SUB, LANES:] for k in range(tiles)]
        ext = [g] + [pltpu.roll(z, FIELDS, 0) for z in across] + [g]
        new = []
        for k in range(tiles):
            vertical = jnp.where(first, ext[k], jnp.where(last, ext[k + 2], ext[k + 1]))
            new.append(x[k] + v * ((flat[k] + across[k]) + vertical))
        return new

    def one(c, _):
        base = pl.multiple_of(c * chunk, chunk)
        x = state[pl.ds(base, chunk)].reshape(chunk * tall, LANES)
        y = dot(x, shift[:LANES])
        xs = []
        gs = []
        for i in range(chunk):
            gs.append(ghosts[strip[base + i]])
            mine = x[i * tall : (i + 1) * tall].astype(F32)
            mine = [mine[k * SUB : (k + 1) * SUB] for k in range(tiles)]
            xs.append(sweep(mine, gs[i], y[i * tall : (i + 1) * tall]))
        for step in range(STEPS - 1):
            flat = jnp.concatenate([z for mine in xs for z in mine], axis=0)
            high = flat.astype(BF16)
            y = dot(jnp.concatenate([high, (flat - high.astype(F32)).astype(BF16)], axis=1), shift[...])
            xs = [sweep(xs[i], gs[i], y[i * tall : (i + 1) * tall]) for i in range(chunk)]
        for i in range(chunk):
            for k in range(tiles):
                done[base + i, k * SUB : (k + 1) * SUB] = xs[i][k]
        pltpu.make_async_copy(done.at[pl.ds(base, chunk)], out.at[pl.ds(base, chunk)], sem).start()
        return 0

    lax.fori_loop(0, count // chunk, one, 0, unroll=count // chunk)
    pltpu.make_async_copy(done, out, sem).wait()


def shift_table():
    table = np.zeros((LANES, 2 * LANES), np.float32)
    for i in range(LANES):
        table[i, i] = -4.0
        for j in (i - 1, i + 1):
            if 0 <= j and j // PC == i // PC:
                table[i, j] = 1.0
        table[i, LANES + (i + PC) % LANES] = 1.0
    return np.concatenate([table, table], axis=0)


def sweeps(strip, state, ghosts, rate):
    vmem = pl.BlockSpec(memory_space=pltpu.VMEM)
    return pl.pallas_call(
        sweep_kernel,
        in_specs=[pl.BlockSpec(memory_space=pltpu.SMEM)] + [vmem] * 4,
        out_specs=pl.BlockSpec(memory_space=pltpu.HBM),
        out_shape=pltpu.HBM(state.shape, F32),
        scratch_shapes=[pltpu.VMEM(state.shape, F32), pltpu.SemaphoreType.DMA],
        compiler_params=pltpu.CompilerParams(vmem_limit_bytes=24 * MIB),
    )(strip, state, ghosts, rate, jnp.asarray(shift_table(), BF16))


def interp_table():
    coarse = PC // 2
    table = np.zeros((2, coarse, 2, PC), np.float32)
    for side in range(2):
        for c in range(PC):
            near = c // 2
            second = max(near - 1, 0) if c % 2 == 0 else min(near + 1, coarse - 1)
            table[side, near, side, c] += 0.75
            table[side, second, side, c] += 0.25
    return table.reshape(2 * coarse, 2 * PC)


def shards(fields, new_owner, leaflet, stiffness, coarse, coarse_of_slot, viscosity):
    devices = lax.axis_size("axial") * lax.axis_size("azim")
    patch_count = fields.shape[0]
    slots = devices * SLOTS_EACH

    leaf, row_one, row_two, sides, target, coupling, spread = first_part(
        leaflet, new_owner.reshape(1, patch_count), stiffness
    )
    side_one = exchange(sides, "azim", 0)
    side_two = exchange(sides, "azim", 1)
    row_one = exchange(row_one, "axial", 0)
    row_two = exchange(row_two, "axial", 1)
    held, lap, sent = laplace(to_tiles(fields), leaf, slots)
    sent, rest = main_part(target, held, lap, spread, sent)
    sent = edge_part(target, rest, coupling, row_one, row_two, side_one, side_two, sent)
    arrived = lax.all_to_all(sent.reshape(devices, -1, LANES), ALL, split_axis=0, concat_axis=0, tiled=True)
    state = arrived.reshape(slots, -1, LANES)

    strips = coarse.shape[0]
    ghosts = jnp.dot(
        coarse.reshape(strips * FIELDS, -1), jnp.asarray(interp_table()), precision=lax.Precision.HIGHEST
    ).reshape(strips, FIELDS, LANES)
    ghosts = jnp.concatenate([ghosts, ghosts], axis=1)
    rate = jnp.broadcast_to(jnp.concatenate([viscosity, viscosity])[:, None], (SUB, LANES))
    return from_tiles(sweeps(coarse_of_slot, state, ghosts, rate))


def solution(mesh):
    placed = (
        P(ALL, None, None),
        P(ALL, None),
        P(None, "axial", "azim"),
        P(),
        P(ALL, None),
        P(ALL),
        P(),
    )
    return jax.shard_map(
        shards,
        mesh=mesh,
        in_specs=placed,
        out_specs=P(ALL, None, None),
        check_vma=False,
    )
```

```python
import jax
import jax.numpy as jnp
import numpy as np
from jax import lax
from jax.experimental import pallas as pl
from jax.experimental.pallas import tpu as pltpu
from jax.sharding import PartitionSpec as P

PC = 64
FIELDS = 4
STEPS = 2
SPREAD = 0.25
LANES = 128
SUB = 8
SLOTS_EACH = 2
ALL = ("axial", "azim")
F32 = jnp.float32
BF16 = jnp.bfloat16
MIB = 2**20


def to_tiles(x):
    n = x.shape[0]
    return x.reshape(n, FIELDS, -1, LANES).transpose(0, 2, 1, 3).reshape(n, -1, LANES)


def from_tiles(x):
    n = x.shape[0]
    return x.reshape(n, -1, FIELDS, LANES).transpose(0, 2, 1, 3).reshape(n, FIELDS, -1)


def iota(shape, dim):
    return lax.broadcasted_iota(jnp.int32, shape, dim)


def dot(a, b):
    return jnp.dot(a, b, preferred_element_type=F32)


def in_hbm(x):
    return pltpu.with_memory_space_constraint(x, pltpu.HBM)


def where_one(mask):
    return jnp.where(mask, 1.0, 0.0).astype(BF16)


def first_kernel(leaf_hbm, leaf, one, two, sides, load_sem):
    records, rows, cols = leaf.shape
    size = 16
    loads = []
    for n in range(records // size):
        part = pl.ds(n * size, size)
        loads.append(pltpu.make_async_copy(leaf_hbm.at[part], leaf.at[part], load_sem.at[n]))
        loads[n].start()

    odd = lax.axis_index("axial") % 2
    a, b = iota((2 * size, size * rows), 0), iota((2 * size, size * rows), 1)
    pick = jnp.where((a // size + odd) % 2 == 0, rows - 1, 0)
    ends = where_one(b == a % size * rows + pick)
    spot = jnp.where(iota((cols, LANES), 1) // rows % 2 == 0, 0, cols - 1)
    spot = where_one(iota((cols, LANES), 0) == spot)
    mine = iota((size * rows, LANES), 1) % rows == iota((size * rows, LANES), 0) % rows
    gather = where_one(iota((size, size * rows), 1) // rows == iota((size, size * rows), 0))
    for n in range(records // size):
        loads[n].wait()
        part = slice(n * size, (n + 1) * size)
        x = leaf[part].reshape(size * rows, cols)
        both = dot(ends, x).astype(BF16)
        one[part] = both[:size]
        two[part] = both[size:]
        sides[part] = dot(gather, jnp.where(mine, dot(x, spot), 0.0).astype(BF16)).astype(BF16)


def first_part(leaf):
    records, rows, cols = leaf.shape
    vmem = pl.BlockSpec(memory_space=pltpu.VMEM)
    shapes = [leaf.shape, (records, cols), (records, cols), (records, LANES)]
    return pl.pallas_call(
        first_kernel,
        in_specs=[pl.BlockSpec(memory_space=pltpu.HBM)],
        out_specs=[vmem] * 4,
        out_shape=[pltpu.VMEM(s, BF16) for s in shapes],
        scratch_shapes=[pltpu.SemaphoreType.DMA((records // 16,))],
        compiler_params=pltpu.CompilerParams(vmem_limit_bytes=16 * MIB),
        cost_estimate=pl.CostEstimate(flops=10**8, bytes_accessed=MIB, transcendentals=0),
    )(in_hbm(leaf))


def exchange(x, axis, offset):
    size = lax.axis_size(axis)
    pairs = [(i % size, (i + 1) % size) for i in range(offset, size + offset, 2)]
    return lax.ppermute(x, axis, pairs + [(j, i) for i, j in pairs])


def halves(a, b, low, t):
    a, b = a[:, t * LANES : (t + 1) * LANES], b[:, t * LANES : (t + 1) * LANES]
    return jnp.where(low, a, pltpu.roll(b, PC, 1)), jnp.where(low, pltpu.roll(a, PC, 1), b)


def edge_patches(rows, quarters):
    return [
        (r, q) for r in range(rows) for q in range(quarters) if r in (0, rows - 1) or q in (0, quarters - 1)
    ]


def main_kernel(
    fields_hbm,
    leaf,
    owner_hbm,
    stiff_hbm,
    image,
    rest,
    target,
    coupling,
    fields,
    lap,
    spread,
    owner,
    stiffness,
    slot,
    load_sem,
    small_sem,
):
    small = [
        pltpu.make_async_copy(owner_hbm, owner, small_sem.at[0]),
        pltpu.make_async_copy(stiff_hbm, stiffness, small_sem.at[1]),
    ]
    for c in small:
        c.start()
    records, rows, cols = leaf.shape
    blocks = rows // SUB
    size = fields.shape[0] // blocks
    loads = []
    for n in range(blocks):
        part = pl.ds(n * size, size)
        loads.append(pltpu.make_async_copy(fields_hbm.at[part], fields.at[part], load_sem.at[n]))
        loads[n].start()

    small[0].wait()
    devices, patches = LANES, owner.shape[1]
    mine = owner[...] == iota((devices, patches), 0)
    before = where_one(iota((patches, patches), 0) < iota((patches, patches), 1))
    earlier = dot(where_one(mine), before)
    ranked = jnp.sum(jnp.where(mine, earlier, 0.0), axis=0, keepdims=True)
    target[...] = owner[...] * SLOTS_EACH + ranked.astype(jnp.int32)

    turn = pltpu.make_async_copy(target, slot, small_sem.at[0])
    turn.start()

    small[1].wait()
    half = records // 2
    a, b = iota((records, records), 0), iota((records, records), 1)
    old = a % FIELDS * (records // FIELDS) + a % half // FIELDS * 2 + a // half
    ordered = (dot(where_one(b == old), stiffness[...]) * SPREAD).astype(BF16)
    coupling[...] = ordered

    wide = records * SUB
    lift = where_one(iota((records, wide), 1) // SUB == iota((records, wide), 0))
    lifted = dot(ordered, lift)
    within = iota((half, wide), 1) % SUB
    for p in range(2):
        for r in range(SUB):
            part = jnp.where(within == r, lifted[p * half : (p + 1) * half], 0.0)
            at = (p * SUB + r) * half
            spread[at : at + half] = part.astype(BF16)

    def clear(i, _):
        image[pl.ds(i * SUB, SUB)] = jnp.zeros((SUB,) + image.shape[1:], BF16)
        return 0

    lax.fori_loop(0, image.shape[0] // SUB, clear, 0)

    group = 256 // rows
    a, b = iota((group * rows, group * rows), 0), iota((group * rows, group * rows), 1)
    beside = where_one((jnp.abs(a - b) == 1) & (a // rows == b // rows))
    a, b = iota((cols, cols), 0), iota((cols, cols), 1)
    along = jnp.where(a == b, -4.0, jnp.where(jnp.abs(a - b) == 1, 1.0, 0.0)).astype(BF16)
    for g in range(records // group):
        x = leaf[g * group : (g + 1) * group].reshape(group * rows, cols)
        y = (dot(beside, x) + dot(x, along)).reshape(group, rows, cols)
        for n in range(rows // SUB):
            part = y[:, n * SUB : (n + 1) * SUB].reshape(group * SUB, cols)
            lap[n, g * group * SUB : (g + 1) * group * SUB] = part.astype(BF16)

    turn.wait()
    quarters = cols // PC
    low = iota((half, LANES), 1) < PC
    edge = {rq: i for i, rq in enumerate(edge_patches(rows, quarters))}
    for n in range(blocks):
        tension = dot(spread[...], lap[n])
        loads[n].wait()
        for k in range(SUB):
            r = n * SUB + k
            a = tension[k * half : (k + 1) * half]
            b = tension[(SUB + k) * half : (SUB + k + 1) * half]
            for t in range(cols // LANES):
                for h, sheet in enumerate(halves(a, b, low, t)):
                    q = 2 * t + h
                    patch = r * quarters + q
                    forced = fields[patch] + sheet
                    if (r, q) in edge:
                        rest[edge[r, q]] = forced
                    else:
                        image[slot[0, patch]] = forced.astype(BF16)


def main_part(fields, leaf, owner, stiffness, slots):
    records, rows, cols = leaf.shape
    _, tall, _ = fields.shape
    vmem = pl.BlockSpec(memory_space=pltpu.VMEM)
    hbm = pl.BlockSpec(memory_space=pltpu.HBM)
    count = len(edge_patches(rows, cols // PC))
    return pl.pallas_call(
        main_kernel,
        in_specs=[hbm, vmem, hbm, hbm],
        out_specs=[vmem] * 4,
        out_shape=[
            pltpu.VMEM((slots, tall, LANES), BF16),
            pltpu.VMEM((count, tall, LANES), F32),
            jax.ShapeDtypeStruct(owner.shape, jnp.int32),
            pltpu.VMEM((records, records), BF16),
        ],
        scratch_shapes=[
            pltpu.VMEM(fields.shape, F32),
            pltpu.VMEM((rows // SUB, records * SUB, cols), BF16),
            pltpu.VMEM((records * SUB, records * SUB), BF16),
            pltpu.VMEM(owner.shape, jnp.int32),
            pltpu.VMEM(stiffness.shape, BF16),
            pltpu.SMEM(owner.shape, jnp.int32),
            pltpu.SemaphoreType.DMA((rows // SUB,)),
            pltpu.SemaphoreType.DMA((2,)),
        ],
        compiler_params=pltpu.CompilerParams(vmem_limit_bytes=16 * MIB),
        cost_estimate=pl.CostEstimate(flops=2 * 10**9, bytes_accessed=8 * MIB, transcendentals=0),
    )(in_hbm(fields), leaf, in_hbm(owner), in_hbm(stiffness))


def edge_kernel(target, rest, coupling, row_two, row_one, side_two, side_one, image_in, image, sent, sem):
    del image_in
    records, cols = row_one.shape
    half = records // 2
    quarters = cols // PC
    rows = LANES // 4
    low = iota((half, LANES), 1) < PC

    lane = iota((records, LANES), 1)
    odd = lax.axis_index("azim") % 2
    near = jnp.where((lane // rows + odd) % 2 == 0, side_one[...].astype(F32), side_two[...].astype(F32)).astype(BF16)
    both = dot(coupling[...], near)
    both = jnp.where(low, both[:half], both[half:])
    lane = iota((half, LANES), 1)
    column = jnp.concatenate([jnp.where(lane % rows == r, both, 0.0) for r in range(rows)], axis=0)
    high = column.astype(BF16)
    split = jnp.concatenate([high, (column - high.astype(F32)).astype(BF16)], axis=1)
    a, b = iota((2 * LANES, 2 * LANES), 0), iota((2 * LANES, 2 * LANES), 1)
    p, s = a // PC % 2, a // rows % 2
    split = dot(split, where_one(b == jnp.where(s == 1, p * PC, LANES + p * PC + PC - 1)))

    place, size = lax.axis_index("axial"), lax.axis_size("axial")
    odd = place % 2 == 1
    one, two = row_one[...].astype(F32), row_two[...].astype(F32)
    two = jnp.where((place == 0) | (place == size - 1), 0.0, two)
    ends = {}
    for r, row in ((0, jnp.where(odd, one, two)), (rows - 1, jnp.where(odd, two, one))):
        whole = dot(coupling[...], row.astype(BF16))
        for t in range(cols // LANES):
            for h, sheet in enumerate(halves(whole[:half], whole[half:], low, t)):
                ends[r, 2 * t + h] = sheet

    listed = edge_patches(rows, quarters)
    for i, (r, q) in enumerate(listed):
        forced = rest[i]
        if q == 0:
            forced = forced + split[r * half : (r + 1) * half, :LANES]
        if q == quarters - 1:
            forced = forced + split[r * half : (r + 1) * half, LANES:]
        if (r, q) in ends:
            forced = forced + ends[r, q]
        image[target[0, r * quarters + q]] = forced.astype(BF16)
    whole = pltpu.make_async_copy(image, sent, sem)
    whole.start()
    whole.wait()


def edge_part(target, rest, coupling, row_two, row_one, side_two, side_one, image):
    vmem = pl.BlockSpec(memory_space=pltpu.VMEM)
    _, sent = pl.pallas_call(
        edge_kernel,
        in_specs=[pl.BlockSpec(memory_space=pltpu.SMEM)] + [vmem] * 7,
        out_specs=[vmem, pl.BlockSpec(memory_space=pltpu.HBM)],
        out_shape=[pltpu.VMEM(image.shape, BF16), pltpu.HBM(image.shape, BF16)],
        scratch_shapes=[pltpu.SemaphoreType.DMA],
        input_output_aliases={7: 0},
        compiler_params=pltpu.CompilerParams(vmem_limit_bytes=16 * MIB),
        cost_estimate=pl.CostEstimate(flops=2 * 10**8, bytes_accessed=2 * MIB, transcendentals=0),
    )(target, rest, coupling, row_two, row_one, side_two, side_one, image)
    return sent


def sweep_kernel(strip, state, ghosts, rate, shift, out, done, sem):
    count, tall, _ = state.shape
    lane = iota((SUB, LANES), 1)
    row = iota((SUB, LANES), 0)
    first = (lane < PC) & (row < FIELDS)
    last = (lane >= PC) & (row >= FIELDS)
    v = rate[...]
    tiles = tall // SUB
    chunk = 8

    def sweep(x, g, y):
        flat = [y[k * SUB : (k + 1) * SUB, :LANES] for k in range(tiles)]
        across = [y[k * SUB : (k + 1) * SUB, LANES:] for k in range(tiles)]
        ext = [g] + [pltpu.roll(z, FIELDS, 0) for z in across] + [g]
        new = []
        for k in range(tiles):
            vertical = jnp.where(first, ext[k], jnp.where(last, ext[k + 2], ext[k + 1]))
            new.append(x[k] + v * ((flat[k] + across[k]) + vertical))
        return new

    def one(c, _):
        base = pl.multiple_of(c * chunk, chunk)
        x = state[pl.ds(base, chunk)].reshape(chunk * tall, LANES)
        y = dot(x, shift[:LANES])
        xs = []
        gs = []
        for i in range(chunk):
            gs.append(ghosts[strip[base + i]])
            mine = x[i * tall : (i + 1) * tall].astype(F32)
            mine = [mine[k * SUB : (k + 1) * SUB] for k in range(tiles)]
            xs.append(sweep(mine, gs[i], y[i * tall : (i + 1) * tall]))
        for step in range(STEPS - 1):
            flat = jnp.concatenate([z for mine in xs for z in mine], axis=0)
            high = flat.astype(BF16)
            y = dot(jnp.concatenate([high, (flat - high.astype(F32)).astype(BF16)], axis=1), shift[...])
            xs = [sweep(xs[i], gs[i], y[i * tall : (i + 1) * tall]) for i in range(chunk)]
        for i in range(chunk):
            for k in range(tiles):
                done[base + i, k * SUB : (k + 1) * SUB] = xs[i][k]
        pltpu.make_async_copy(done.at[pl.ds(base, chunk)], out.at[pl.ds(base, chunk)], sem).start()
        return 0

    lax.fori_loop(0, count // chunk, one, 0, unroll=count // chunk)
    pltpu.make_async_copy(done, out, sem).wait()


def shift_table():
    table = np.zeros((LANES, 2 * LANES), np.float32)
    for i in range(LANES):
        table[i, i] = -4.0
        for j in (i - 1, i + 1):
            if 0 <= j and j // PC == i // PC:
                table[i, j] = 1.0
        table[i, LANES + (i + PC) % LANES] = 1.0
    return np.concatenate([table, table], axis=0)


def sweeps(strip, state, ghosts, rate):
    vmem = pl.BlockSpec(memory_space=pltpu.VMEM)
    return pl.pallas_call(
        sweep_kernel,
        in_specs=[pl.BlockSpec(memory_space=pltpu.SMEM)] + [vmem] * 4,
        out_specs=pl.BlockSpec(memory_space=pltpu.HBM),
        out_shape=pltpu.HBM(state.shape, F32),
        scratch_shapes=[pltpu.VMEM(state.shape, F32), pltpu.SemaphoreType.DMA],
        compiler_params=pltpu.CompilerParams(vmem_limit_bytes=24 * MIB),
    )(strip, state, ghosts, rate, jnp.asarray(shift_table(), BF16))


def interp_table():
    coarse = PC // 2
    table = np.zeros((2, coarse, 2, PC), np.float32)
    for side in range(2):
        for c in range(PC):
            near = c // 2
            second = max(near - 1, 0) if c % 2 == 0 else min(near + 1, coarse - 1)
            table[side, near, side, c] += 0.75
            table[side, second, side, c] += 0.25
    return table.reshape(2 * coarse, 2 * PC)


def shards(fields, new_owner, leaflet, stiffness, coarse, coarse_of_slot, viscosity):
    devices = lax.axis_size("axial") * lax.axis_size("azim")
    patch_count = fields.shape[0]
    slots = devices * SLOTS_EACH

    leaf, row_one, row_two, sides = first_part(leaflet)
    side_two = exchange(sides, "azim", 1)
    side_one = exchange(sides, "azim", 0)
    row_two = exchange(row_two, "axial", 1)
    row_one = exchange(row_one, "axial", 0)
    image, rest, target, coupling = main_part(to_tiles(fields), leaf, new_owner.reshape(1, patch_count), stiffness, slots)
    sent = edge_part(target, rest, coupling, row_two, row_one, side_two, side_one, image)
    arrived = lax.all_to_all(sent.reshape(devices, -1, LANES), ALL, split_axis=0, concat_axis=0, tiled=True)
    state = arrived.reshape(slots, -1, LANES)

    strips = coarse.shape[0]
    ghosts = jnp.dot(
        coarse.reshape(strips * FIELDS, -1), jnp.asarray(interp_table()), precision=lax.Precision.HIGHEST
    ).reshape(strips, FIELDS, LANES)
    ghosts = jnp.concatenate([ghosts, ghosts], axis=1)
    rate = jnp.broadcast_to(jnp.concatenate([viscosity, viscosity])[:, None], (SUB, LANES))
    return from_tiles(sweeps(coarse_of_slot, state, ghosts, rate))


def solution(mesh):
    placed = (
        P(ALL, None, None),
        P(ALL, None),
        P(None, "axial", "azim"),
        P(),
        P(ALL, None),
        P(ALL),
        P(),
    )
    return jax.shard_map(
        shards,
        mesh=mesh,
        in_specs=placed,
        out_specs=P(ALL, None, None),
        check_vma=False,
    )
```

```python
import jax
import jax.numpy as jnp
import numpy as np
from jax import lax
from jax.experimental import pallas as pl
from jax.experimental.pallas import tpu as pltpu
from jax.sharding import PartitionSpec as P

PC = 64
FIELDS = 4
STEPS = 2
SPREAD = 0.25
LANES = 128
SUB = 8
SLOTS_EACH = 2
ALL = ("axial", "azim")
F32 = jnp.float32
BF16 = jnp.bfloat16
MIB = 2**20


def to_tiles(x):
    n = x.shape[0]
    return x.reshape(n, FIELDS, -1, LANES).transpose(0, 2, 1, 3).reshape(n, -1, LANES)


def from_tiles(x):
    n = x.shape[0]
    return x.reshape(n, -1, FIELDS, LANES).transpose(0, 2, 1, 3).reshape(n, FIELDS, -1)


def iota(shape, dim):
    return lax.broadcasted_iota(jnp.int32, shape, dim)


def dot(a, b):
    return jnp.dot(a, b, preferred_element_type=F32)


def in_hbm(x):
    return pltpu.with_memory_space_constraint(x, pltpu.HBM)


def in_vmem(x):
    return pltpu.with_memory_space_constraint(x, pltpu.VMEM)


def where_one(mask):
    return jnp.where(mask, 1.0, 0.0).astype(BF16)


def first_kernel(leaf, one, two, sides):
    records, rows, cols = leaf.shape
    half = rows // 2
    odd = lax.axis_index("axial") % 2
    spot = jnp.where(iota((cols, LANES), 1) // rows % 2 == 0, 0, cols - 1)
    wide = dot(leaf[...].reshape(-1, cols), where_one(iota((cols, LANES), 0) == spot))
    r = iota((records * rows, LANES), 0) % rows
    wide = jnp.where(iota((records * rows, LANES), 1) % rows == r, wide, 0.0).astype(BF16)
    gather = iota((records, records * rows), 1) // rows == iota((records, records * rows), 0)
    sides[...] = dot(where_one(gather), wide).astype(BF16)
    pick = iota((records, records * half), 1) - iota((records, records * half), 0) * half
    first = dot(where_one(pick == 0), leaf[:, :half].reshape(-1, cols))
    last = dot(where_one(pick == half - 1), leaf[:, half:].reshape(-1, cols))
    one[...] = jnp.where(odd == 0, last, first).astype(BF16)
    two[...] = jnp.where(odd == 0, first, last).astype(BF16)


def first_part(leaf):
    records, rows, cols = leaf.shape
    vmem = pl.BlockSpec(memory_space=pltpu.VMEM)
    shapes = [(records, cols), (records, cols), (records, LANES)]
    return pl.pallas_call(
        first_kernel,
        in_specs=[vmem],
        out_specs=[vmem] * 3,
        out_shape=[pltpu.VMEM(s, BF16) for s in shapes],
        compiler_params=pltpu.CompilerParams(vmem_limit_bytes=16 * MIB),
        cost_estimate=pl.CostEstimate(flops=10**8, bytes_accessed=MIB, transcendentals=0),
    )(leaf)


def laplace_kernel(
    leaf, owner_hbm, stiff_hbm, lap, sent, target, coupling, spread, zero, owner, stiffness, zero_sem, small_sem
):
    small = [
        pltpu.make_async_copy(owner_hbm, owner, small_sem.at[0]),
        pltpu.make_async_copy(stiff_hbm, stiffness, small_sem.at[1]),
    ]
    for c in small:
        c.start()
    zero[...] = jnp.zeros_like(zero)
    count = zero.shape[0]
    clears = [
        pltpu.make_async_copy(zero, sent.at[pl.ds(i * count, count)], zero_sem) for i in range(sent.shape[0] // count)
    ]
    for c in clears:
        c.start()
    records, rows, cols = leaf.shape

    group = 256 // rows
    a, b = iota((group * rows, group * rows), 0), iota((group * rows, group * rows), 1)
    beside = where_one((jnp.abs(a - b) == 1) & (a // rows == b // rows))
    a, b = iota((cols, cols), 0), iota((cols, cols), 1)
    along = jnp.where(a == b, -4.0, jnp.where(jnp.abs(a - b) == 1, 1.0, 0.0)).astype(BF16)
    for g in range(records // group):
        x = leaf[g * group : (g + 1) * group].reshape(group * rows, cols)
        y = (dot(beside, x) + dot(x, along)).reshape(group, rows, cols)
        for n in range(rows // SUB):
            part = y[:, n * SUB : (n + 1) * SUB].reshape(group * SUB, cols)
            lap[n, g * group * SUB : (g + 1) * group * SUB] = part.astype(BF16)
    small[0].wait()
    devices, patches = LANES, owner.shape[1]
    mine = owner[...] == iota((devices, patches), 0)
    before = where_one(iota((patches, patches), 0) < iota((patches, patches), 1))
    earlier = dot(where_one(mine), before)
    ranked = jnp.sum(jnp.where(mine, earlier, 0.0), axis=0, keepdims=True)
    target[...] = owner[...] * SLOTS_EACH + ranked.astype(jnp.int32)

    small[1].wait()
    half = records // 2
    a, b = iota((records, records), 0), iota((records, records), 1)
    old = a % FIELDS * (records // FIELDS) + a % half // FIELDS * 2 + a // half
    ordered = (dot(where_one(b == old), stiffness[...]) * SPREAD).astype(BF16)
    coupling[...] = ordered

    wide = records * SUB
    lift = where_one(iota((records, wide), 1) // SUB == iota((records, wide), 0))
    lifted = dot(ordered, lift)
    within = iota((half, wide), 1) % SUB
    for p in range(2):
        for r in range(SUB):
            part = jnp.where(within == r, lifted[p * half : (p + 1) * half], 0.0)
            at = (p * SUB + r) * half
            spread[at : at + half] = part.astype(BF16)
    for c in clears:
        c.wait()


def laplace(leaf, owner, stiffness, slots):
    records, rows, cols = leaf.shape
    vmem = pl.BlockSpec(memory_space=pltpu.VMEM)
    hbm = pl.BlockSpec(memory_space=pltpu.HBM)
    tile = (records // 2, LANES)
    return pl.pallas_call(
        laplace_kernel,
        in_specs=[vmem, hbm, hbm],
        out_specs=[vmem, hbm, vmem, vmem, vmem],
        out_shape=[
            pltpu.VMEM((rows // SUB, records * SUB, cols), BF16),
            pltpu.HBM((slots,) + tile, BF16),
            jax.ShapeDtypeStruct(owner.shape, jnp.int32),
            pltpu.VMEM((records, records), BF16),
            pltpu.VMEM((records * SUB, records * SUB), BF16),
        ],
        scratch_shapes=[
            pltpu.VMEM((32,) + tile, BF16),
            pltpu.VMEM(owner.shape, jnp.int32),
            pltpu.VMEM(stiffness.shape, BF16),
            pltpu.SemaphoreType.DMA,
            pltpu.SemaphoreType.DMA((2,)),
        ],
        compiler_params=pltpu.CompilerParams(vmem_limit_bytes=16 * MIB),
        cost_estimate=pl.CostEstimate(flops=5 * 10**8, bytes_accessed=3 * MIB, transcendentals=0),
    )(leaf, in_hbm(owner), in_hbm(stiffness))


def exchange(x, axis, offset):
    size = lax.axis_size(axis)
    pairs = [(i % size, (i + 1) % size) for i in range(offset, size + offset, 2)]
    return lax.ppermute(x, axis, pairs + [(j, i) for i, j in pairs])


def halves(a, b, low, t):
    a, b = a[:, t * LANES : (t + 1) * LANES], b[:, t * LANES : (t + 1) * LANES]
    return jnp.where(low, a, pltpu.roll(b, PC, 1)), jnp.where(low, pltpu.roll(a, PC, 1), b)


def edge_patches(rows, quarters):
    return [
        (r, q) for r in range(rows) for q in range(quarters) if r in (0, rows - 1) or q in (0, quarters - 1)
    ]


def main_kernel(target, fields, lap, spread, sent_in, sent, rest, stage, sem):
    del sent_in
    blocks, _, cols = lap.shape
    half = fields.shape[1]
    rows = blocks * SUB
    quarters = cols // PC
    low = iota((half, LANES), 1) < PC
    listed = edge_patches(rows, quarters)
    edge = {rq: i for i, rq in enumerate(listed)}
    for n in range(blocks):
        tension = dot(spread[...], lap[n])
        for k in range(SUB):
            r = n * SUB + k
            a = tension[k * half : (k + 1) * half]
            b = tension[(SUB + k) * half : (SUB + k + 1) * half]
            for t in range(cols // LANES):
                for h, sheet in enumerate(halves(a, b, low, t)):
                    q = 2 * t + h
                    patch = r * quarters + q
                    forced = fields[patch] + sheet
                    if (r, q) in edge:
                        rest[edge[r, q]] = forced
                    else:
                        stage[patch] = forced.astype(BF16)
                        pltpu.make_async_copy(stage.at[patch], sent.at[target[0, patch]], sem).start()
    count = rows * quarters - len(edge)
    pltpu.make_async_copy(stage.at[pl.ds(0, count)], sent.at[pl.ds(0, count)], sem).wait()


def main_part(target, fields, lap, spread, sent):
    patches, tall, _ = fields.shape
    blocks, _, cols = lap.shape
    vmem = pl.BlockSpec(memory_space=pltpu.VMEM)
    hbm = pl.BlockSpec(memory_space=pltpu.HBM)
    count = len(edge_patches(blocks * SUB, cols // PC))
    return pl.pallas_call(
        main_kernel,
        in_specs=[pl.BlockSpec(memory_space=pltpu.SMEM), vmem, vmem, vmem, hbm],
        out_specs=[hbm, vmem],
        out_shape=[pltpu.HBM(sent.shape, BF16), pltpu.VMEM((count, tall, LANES), F32)],
        scratch_shapes=[pltpu.VMEM((patches, tall, LANES), BF16), pltpu.SemaphoreType.DMA],
        input_output_aliases={4: 0},
        compiler_params=pltpu.CompilerParams(vmem_limit_bytes=16 * MIB),
        cost_estimate=pl.CostEstimate(flops=10**9, bytes_accessed=4 * MIB, transcendentals=0),
    )(target, fields, lap, spread, sent)


def edge_kernel(target, rest, coupling, row_two, row_one, side_two, side_one, sent_in, sent, stage, sem):
    del sent_in
    records, cols = row_one.shape
    half = records // 2
    quarters = cols // PC
    rows = LANES // 4
    low = iota((half, LANES), 1) < PC

    lane = iota((records, LANES), 1)
    odd = lax.axis_index("azim") % 2
    near = jnp.where((lane // rows + odd) % 2 == 0, side_one[...].astype(F32), side_two[...].astype(F32)).astype(BF16)
    both = dot(coupling[...], near)
    both = jnp.where(low, both[:half], both[half:])
    lane = iota((half, LANES), 1)
    column = jnp.concatenate([jnp.where(lane % rows == r, both, 0.0) for r in range(rows)], axis=0)
    high = column.astype(BF16)
    split = jnp.concatenate([high, (column - high.astype(F32)).astype(BF16)], axis=1)
    a, b = iota((2 * LANES, 2 * LANES), 0), iota((2 * LANES, 2 * LANES), 1)
    p, s = a // PC % 2, a // rows % 2
    split = dot(split, where_one(b == jnp.where(s == 1, p * PC, LANES + p * PC + PC - 1)))

    place, size = lax.axis_index("axial"), lax.axis_size("axial")
    odd = place % 2 == 1
    one, two = row_one[...].astype(F32), row_two[...].astype(F32)
    two = jnp.where((place == 0) | (place == size - 1), 0.0, two)
    ends = {}
    for r, row in ((0, jnp.where(odd, one, two)), (rows - 1, jnp.where(odd, two, one))):
        whole = dot(coupling[...], row.astype(BF16))
        for t in range(cols // LANES):
            for h, sheet in enumerate(halves(whole[:half], whole[half:], low, t)):
                ends[r, 2 * t + h] = sheet

    listed = edge_patches(rows, quarters)
    for i, (r, q) in enumerate(listed):
        forced = rest[i]
        if q == 0:
            forced = forced + split[r * half : (r + 1) * half, :LANES]
        if q == quarters - 1:
            forced = forced + split[r * half : (r + 1) * half, LANES:]
        if (r, q) in ends:
            forced = forced + ends[r, q]
        stage[i] = forced.astype(BF16)
        pltpu.make_async_copy(stage.at[i], sent.at[target[0, r * quarters + q]], sem).start()
    count = len(listed)
    pltpu.make_async_copy(stage, sent.at[pl.ds(0, count)], sem).wait()


def edge_part(target, rest, coupling, row_two, row_one, side_two, side_one, sent):
    vmem = pl.BlockSpec(memory_space=pltpu.VMEM)
    return pl.pallas_call(
        edge_kernel,
        in_specs=[pl.BlockSpec(memory_space=pltpu.SMEM)] + [vmem] * 6 + [pl.BlockSpec(memory_space=pltpu.HBM)],
        out_specs=pl.BlockSpec(memory_space=pltpu.HBM),
        out_shape=pltpu.HBM(sent.shape, sent.dtype),
        scratch_shapes=[pltpu.VMEM(rest.shape, BF16), pltpu.SemaphoreType.DMA],
        input_output_aliases={7: 0},
        compiler_params=pltpu.CompilerParams(vmem_limit_bytes=16 * MIB),
        cost_estimate=pl.CostEstimate(flops=2 * 10**8, bytes_accessed=2 * MIB, transcendentals=0),
    )(target, rest, coupling, row_two, row_one, side_two, side_one, sent)


def sweep_kernel(strip, state, ghosts, rate, shift, out, done, sem):
    count, tall, _ = state.shape
    lane = iota((SUB, LANES), 1)
    row = iota((SUB, LANES), 0)
    first = (lane < PC) & (row < FIELDS)
    last = (lane >= PC) & (row >= FIELDS)
    v = rate[...]
    tiles = tall // SUB
    chunk = 8

    def sweep(x, g, y):
        flat = [y[k * SUB : (k + 1) * SUB, :LANES] for k in range(tiles)]
        across = [y[k * SUB : (k + 1) * SUB, LANES:] for k in range(tiles)]
        ext = [g] + [pltpu.roll(z, FIELDS, 0) for z in across] + [g]
        new = []
        for k in range(tiles):
            vertical = jnp.where(first, ext[k], jnp.where(last, ext[k + 2], ext[k + 1]))
            new.append(x[k] + v * (flat[k] + vertical))
        return new

    def one(c, _):
        base = pl.multiple_of(c * chunk, chunk)
        x = state[pl.ds(base, chunk)].reshape(chunk * tall, LANES)
        y = dot(x, shift[:LANES])
        xs = []
        gs = []
        for i in range(chunk):
            gs.append(ghosts[strip[base + i]])
            mine = x[i * tall : (i + 1) * tall].astype(F32)
            mine = [mine[k * SUB : (k + 1) * SUB] for k in range(tiles)]
            xs.append(sweep(mine, gs[i], y[i * tall : (i + 1) * tall]))
        for step in range(STEPS - 1):
            flat = jnp.concatenate([z for mine in xs for z in mine], axis=0)
            high = flat.astype(BF16)
            y = dot(jnp.concatenate([high, (flat - high.astype(F32)).astype(BF16)], axis=1), shift[...])
            xs = [sweep(xs[i], gs[i], y[i * tall : (i + 1) * tall]) for i in range(chunk)]
        for i in range(chunk):
            for k in range(tiles):
                done[base + i, k * SUB : (k + 1) * SUB] = xs[i][k]
        pltpu.make_async_copy(done.at[pl.ds(base, chunk)], out.at[pl.ds(base, chunk)], sem).start()
        return 0

    lax.fori_loop(0, count // chunk, one, 0, unroll=count // chunk)
    pltpu.make_async_copy(done, out, sem).wait()


def shift_table():
    table = np.zeros((LANES, 2 * LANES), np.float32)
    for i in range(LANES):
        table[i, i] = -4.0
        for j in (i - 1, i + 1):
            if 0 <= j and j // PC == i // PC:
                table[i, j] = 1.0
        table[i, (i + PC) % LANES] = 1.0
        table[i, LANES + (i + PC) % LANES] = 1.0
    return np.concatenate([table, table], axis=0)


def sweeps(strip, state, ghosts, rate):
    vmem = pl.BlockSpec(memory_space=pltpu.VMEM)
    return pl.pallas_call(
        sweep_kernel,
        in_specs=[pl.BlockSpec(memory_space=pltpu.SMEM)] + [vmem] * 4,
        out_specs=pl.BlockSpec(memory_space=pltpu.HBM),
        out_shape=pltpu.HBM(state.shape, F32),
        scratch_shapes=[pltpu.VMEM(state.shape, F32), pltpu.SemaphoreType.DMA],
        compiler_params=pltpu.CompilerParams(vmem_limit_bytes=24 * MIB),
    )(strip, state, ghosts, rate, jnp.asarray(shift_table(), BF16))


def interp_table():
    coarse = PC // 2
    table = np.zeros((2, coarse, 2, PC), np.float32)
    for side in range(2):
        for c in range(PC):
            near = c // 2
            second = max(near - 1, 0) if c % 2 == 0 else min(near + 1, coarse - 1)
            table[side, near, side, c] += 0.75
            table[side, second, side, c] += 0.25
    return table.reshape(2 * coarse, 2 * PC)


def shards(fields, new_owner, leaflet, stiffness, coarse, coarse_of_slot, viscosity):
    devices = lax.axis_size("axial") * lax.axis_size("azim")
    patch_count = fields.shape[0]
    slots = devices * SLOTS_EACH

    leaf = in_vmem(leaflet)
    row_one, row_two, sides = first_part(leaf)
    side_two = exchange(sides, "azim", 1)
    side_one = exchange(sides, "azim", 0)
    row_two = exchange(row_two, "axial", 1)
    row_one = exchange(row_one, "axial", 0)
    lap, sent, target, coupling, spread = laplace(leaf, new_owner.reshape(1, patch_count), stiffness, slots)
    held = in_vmem(to_tiles(fields))
    sent, rest = main_part(target, held, lap, spread, sent)
    sent = edge_part(target, rest, coupling, row_two, row_one, side_two, side_one, sent)
    arrived = lax.all_to_all(sent.reshape(devices, -1, LANES), ALL, split_axis=0, concat_axis=0, tiled=True)
    state = arrived.reshape(slots, -1, LANES)

    strips = coarse.shape[0]
    ghosts = jnp.dot(
        coarse.reshape(strips * FIELDS, -1), jnp.asarray(interp_table()), precision=lax.Precision.HIGHEST
    ).reshape(strips, FIELDS, LANES)
    ghosts = jnp.concatenate([ghosts, ghosts], axis=1)
    rate = jnp.broadcast_to(jnp.concatenate([viscosity, viscosity])[:, None], (SUB, LANES))
    return from_tiles(sweeps(coarse_of_slot, state, ghosts, rate))


def solution(mesh):
    placed = (
        P(ALL, None, None),
        P(ALL, None),
        P(None, "axial", "azim"),
        P(),
        P(ALL, None),
        P(ALL),
        P(),
    )
    return jax.shard_map(
        shards,
        mesh=mesh,
        in_specs=placed,
        out_specs=P(ALL, None, None),
        check_vma=False,
    )
```

```python
import jax
import jax.numpy as jnp
import numpy as np
from jax import lax
from jax.experimental import pallas as pl
from jax.experimental.pallas import tpu as pltpu
from jax.sharding import PartitionSpec as P

PC = 64
FIELDS = 4
STEPS = 2
SPREAD = 0.25
LANES = 128
SUB = 8
SLOTS_EACH = 2
ALL = ("axial", "azim")
F32 = jnp.float32
BF16 = jnp.bfloat16
MIB = 2**20


def to_tiles(x):
    n = x.shape[0]
    return x.reshape(n, FIELDS, -1, LANES).transpose(0, 2, 1, 3).reshape(n, -1, LANES)


def from_tiles(x):
    n = x.shape[0]
    return x.reshape(n, -1, FIELDS, LANES).transpose(0, 2, 1, 3).reshape(n, FIELDS, -1)


def iota(shape, dim):
    return lax.broadcasted_iota(jnp.int32, shape, dim)


def dot(a, b):
    return jnp.dot(a, b, preferred_element_type=F32)


def in_hbm(x):
    return pltpu.with_memory_space_constraint(x, pltpu.HBM)


def in_vmem(x):
    return pltpu.with_memory_space_constraint(x, pltpu.VMEM)


def where_one(mask):
    return jnp.where(mask, 1.0, 0.0).astype(BF16)


def first_kernel(leaf, one, two, sides):
    records, rows, cols = leaf.shape
    half = rows // 2
    odd = lax.axis_index("axial") % 2
    spot = jnp.where(iota((cols, LANES), 1) // rows % 2 == 0, 0, cols - 1)
    wide = dot(leaf[...].reshape(-1, cols), where_one(iota((cols, LANES), 0) == spot))
    r = iota((records * rows, LANES), 0) % rows
    wide = jnp.where(iota((records * rows, LANES), 1) % rows == r, wide, 0.0).astype(BF16)
    gather = iota((records, records * rows), 1) // rows == iota((records, records * rows), 0)
    sides[...] = dot(where_one(gather), wide).astype(BF16)
    pick = iota((records, records * half), 1) - iota((records, records * half), 0) * half
    first = dot(where_one(pick == 0), leaf[:, :half].reshape(-1, cols))
    last = dot(where_one(pick == half - 1), leaf[:, half:].reshape(-1, cols))
    one[...] = jnp.where(odd == 0, last, first).astype(BF16)
    two[...] = jnp.where(odd == 0, first, last).astype(BF16)


def first_part(leaf):
    records, rows, cols = leaf.shape
    vmem = pl.BlockSpec(memory_space=pltpu.VMEM)
    shapes = [(records, cols), (records, cols), (records, LANES)]
    return pl.pallas_call(
        first_kernel,
        in_specs=[vmem],
        out_specs=[vmem] * 3,
        out_shape=[pltpu.VMEM(s, BF16) for s in shapes],
        compiler_params=pltpu.CompilerParams(vmem_limit_bytes=16 * MIB),
        cost_estimate=pl.CostEstimate(flops=10**8, bytes_accessed=MIB, transcendentals=0),
    )(leaf)


def laplace_kernel(
    leaf, owner_hbm, stiff_hbm, lap, target, coupling, spread, owner, stiffness, small_sem
):
    small = [
        pltpu.make_async_copy(owner_hbm, owner, small_sem.at[0]),
        pltpu.make_async_copy(stiff_hbm, stiffness, small_sem.at[1]),
    ]
    for c in small:
        c.start()
    records, rows, cols = leaf.shape

    group = 256 // rows
    a, b = iota((group * rows, group * rows), 0), iota((group * rows, group * rows), 1)
    beside = where_one((jnp.abs(a - b) == 1) & (a // rows == b // rows))
    a, b = iota((cols, cols), 0), iota((cols, cols), 1)
    along = jnp.where(a == b, -4.0, jnp.where(jnp.abs(a - b) == 1, 1.0, 0.0)).astype(BF16)
    for g in range(records // group):
        x = leaf[g * group : (g + 1) * group].reshape(group * rows, cols)
        y = (dot(beside, x) + dot(x, along)).reshape(group, rows, cols)
        for n in range(rows // SUB):
            part = y[:, n * SUB : (n + 1) * SUB].reshape(group * SUB, cols)
            lap[n, g * group * SUB : (g + 1) * group * SUB] = part.astype(BF16)
    small[0].wait()
    devices, patches = LANES, owner.shape[1]
    mine = owner[...] == iota((devices, patches), 0)
    before = where_one(iota((patches, patches), 0) < iota((patches, patches), 1))
    earlier = dot(where_one(mine), before)
    ranked = jnp.sum(jnp.where(mine, earlier, 0.0), axis=0, keepdims=True)
    target[...] = owner[...] * SLOTS_EACH + ranked.astype(jnp.int32)

    small[1].wait()
    half = records // 2
    a, b = iota((records, records), 0), iota((records, records), 1)
    old = a % FIELDS * (records // FIELDS) + a % half // FIELDS * 2 + a // half
    ordered = (dot(where_one(b == old), stiffness[...]) * SPREAD).astype(BF16)
    coupling[...] = ordered

    wide = records * SUB
    lift = where_one(iota((records, wide), 1) // SUB == iota((records, wide), 0))
    lifted = dot(ordered, lift)
    within = iota((half, wide), 1) % SUB
    for p in range(2):
        for r in range(SUB):
            part = jnp.where(within == r, lifted[p * half : (p + 1) * half], 0.0)
            at = (p * SUB + r) * half
            spread[at : at + half] = part.astype(BF16)


def laplace(leaf, owner, stiffness):
    records, rows, cols = leaf.shape
    vmem = pl.BlockSpec(memory_space=pltpu.VMEM)
    hbm = pl.BlockSpec(memory_space=pltpu.HBM)
    return pl.pallas_call(
        laplace_kernel,
        in_specs=[vmem, hbm, hbm],
        out_specs=[vmem] * 4,
        out_shape=[
            pltpu.VMEM((rows // SUB, records * SUB, cols), BF16),
            jax.ShapeDtypeStruct(owner.shape, jnp.int32),
            pltpu.VMEM((records, records), BF16),
            pltpu.VMEM((records * SUB, records * SUB), BF16),
        ],
        scratch_shapes=[
            pltpu.VMEM(owner.shape, jnp.int32),
            pltpu.VMEM(stiffness.shape, BF16),
            pltpu.SemaphoreType.DMA((2,)),
        ],
        compiler_params=pltpu.CompilerParams(vmem_limit_bytes=16 * MIB),
        cost_estimate=pl.CostEstimate(flops=5 * 10**8, bytes_accessed=3 * MIB, transcendentals=0),
    )(leaf, in_hbm(owner), in_hbm(stiffness))


def exchange(x, axis, offset):
    size = lax.axis_size(axis)
    pairs = [(i % size, (i + 1) % size) for i in range(offset, size + offset, 2)]
    return lax.ppermute(x, axis, pairs + [(j, i) for i, j in pairs])


def halves(a, b, low, t):
    a, b = a[:, t * LANES : (t + 1) * LANES], b[:, t * LANES : (t + 1) * LANES]
    return jnp.where(low, a, pltpu.roll(b, PC, 1)), jnp.where(low, pltpu.roll(a, PC, 1), b)


def edge_patches(rows, quarters):
    return [
        (r, q) for r in range(rows) for q in range(quarters) if r in (0, rows - 1) or q in (0, quarters - 1)
    ]


def main_kernel(target, fields, lap, spread, image, rest):
    blocks, _, cols = lap.shape
    half = fields.shape[1]
    rows = blocks * SUB
    quarters = cols // PC
    low = iota((half, LANES), 1) < PC
    edge = {rq: i for i, rq in enumerate(edge_patches(rows, quarters))}
    image[...] = jnp.zeros_like(image)
    for n in range(blocks):
        tension = dot(spread[...], lap[n])
        for k in range(SUB):
            r = n * SUB + k
            a = tension[k * half : (k + 1) * half]
            b = tension[(SUB + k) * half : (SUB + k + 1) * half]
            for t in range(cols // LANES):
                for h, sheet in enumerate(halves(a, b, low, t)):
                    q = 2 * t + h
                    patch = r * quarters + q
                    forced = fields[patch] + sheet
                    if (r, q) in edge:
                        rest[edge[r, q]] = forced
                    else:
                        image[target[0, patch]] = forced.astype(BF16)


def main_part(target, fields, lap, spread, slots):
    _, tall, _ = fields.shape
    blocks, _, cols = lap.shape
    vmem = pl.BlockSpec(memory_space=pltpu.VMEM)
    count = len(edge_patches(blocks * SUB, cols // PC))
    return pl.pallas_call(
        main_kernel,
        in_specs=[pl.BlockSpec(memory_space=pltpu.SMEM), vmem, vmem, vmem],
        out_specs=[vmem, vmem],
        out_shape=[pltpu.VMEM((slots, tall, LANES), BF16), pltpu.VMEM((count, tall, LANES), F32)],
        compiler_params=pltpu.CompilerParams(vmem_limit_bytes=16 * MIB),
        cost_estimate=pl.CostEstimate(flops=10**9, bytes_accessed=4 * MIB, transcendentals=0),
    )(target, fields, lap, spread)


def edge_kernel(target, rest, coupling, row_two, row_one, side_two, side_one, image_in, image, sent, sem):
    del image_in
    records, cols = row_one.shape
    half = records // 2
    quarters = cols // PC
    rows = LANES // 4
    low = iota((half, LANES), 1) < PC

    lane = iota((records, LANES), 1)
    odd = lax.axis_index("azim") % 2
    near = jnp.where((lane // rows + odd) % 2 == 0, side_one[...].astype(F32), side_two[...].astype(F32)).astype(BF16)
    both = dot(coupling[...], near)
    both = jnp.where(low, both[:half], both[half:])
    lane = iota((half, LANES), 1)
    column = jnp.concatenate([jnp.where(lane % rows == r, both, 0.0) for r in range(rows)], axis=0)
    high = column.astype(BF16)
    split = jnp.concatenate([high, (column - high.astype(F32)).astype(BF16)], axis=1)
    a, b = iota((2 * LANES, 2 * LANES), 0), iota((2 * LANES, 2 * LANES), 1)
    p, s = a // PC % 2, a // rows % 2
    split = dot(split, where_one(b == jnp.where(s == 1, p * PC, LANES + p * PC + PC - 1)))

    place, size = lax.axis_index("axial"), lax.axis_size("axial")
    odd = place % 2 == 1
    one, two = row_one[...].astype(F32), row_two[...].astype(F32)
    two = jnp.where((place == 0) | (place == size - 1), 0.0, two)
    ends = {}
    for r, row in ((0, jnp.where(odd, one, two)), (rows - 1, jnp.where(odd, two, one))):
        whole = dot(coupling[...], row.astype(BF16))
        for t in range(cols // LANES):
            for h, sheet in enumerate(halves(whole[:half], whole[half:], low, t)):
                ends[r, 2 * t + h] = sheet

    listed = edge_patches(rows, quarters)
    for i, (r, q) in enumerate(listed):
        forced = rest[i]
        if q == 0:
            forced = forced + split[r * half : (r + 1) * half, :LANES]
        if q == quarters - 1:
            forced = forced + split[r * half : (r + 1) * half, LANES:]
        if (r, q) in ends:
            forced = forced + ends[r, q]
        image[target[0, r * quarters + q]] = forced.astype(BF16)
    whole = pltpu.make_async_copy(image, sent, sem)
    whole.start()
    whole.wait()


def edge_part(target, rest, coupling, row_two, row_one, side_two, side_one, image):
    vmem = pl.BlockSpec(memory_space=pltpu.VMEM)
    _, sent = pl.pallas_call(
        edge_kernel,
        in_specs=[pl.BlockSpec(memory_space=pltpu.SMEM)] + [vmem] * 7,
        out_specs=[vmem, pl.BlockSpec(memory_space=pltpu.HBM)],
        out_shape=[pltpu.VMEM(image.shape, BF16), pltpu.HBM(image.shape, BF16)],
        scratch_shapes=[pltpu.SemaphoreType.DMA],
        input_output_aliases={7: 0},
        compiler_params=pltpu.CompilerParams(vmem_limit_bytes=16 * MIB),
        cost_estimate=pl.CostEstimate(flops=2 * 10**8, bytes_accessed=2 * MIB, transcendentals=0),
    )(target, rest, coupling, row_two, row_one, side_two, side_one, image)
    return sent


def sweep_kernel(strip, state, ghosts, rate, shift, out, done, sem):
    count, tall, _ = state.shape
    lane = iota((SUB, LANES), 1)
    row = iota((SUB, LANES), 0)
    first = (lane < PC) & (row < FIELDS)
    last = (lane >= PC) & (row >= FIELDS)
    v = rate[...]
    tiles = tall // SUB
    chunk = 8

    def sweep(x, g, y):
        flat = [y[k * SUB : (k + 1) * SUB, :LANES] for k in range(tiles)]
        across = [y[k * SUB : (k + 1) * SUB, LANES:] for k in range(tiles)]
        ext = [g] + [pltpu.roll(z, FIELDS, 0) for z in across] + [g]
        new = []
        for k in range(tiles):
            vertical = jnp.where(first, ext[k], jnp.where(last, ext[k + 2], ext[k + 1]))
            new.append(x[k] + v * (flat[k] + vertical))
        return new

    def one(c, _):
        base = pl.multiple_of(c * chunk, chunk)
        x = state[pl.ds(base, chunk)].reshape(chunk * tall, LANES)
        y = dot(x, shift[:LANES])
        xs = []
        gs = []
        for i in range(chunk):
            gs.append(ghosts[strip[base + i]])
            mine = x[i * tall : (i + 1) * tall].astype(F32)
            mine = [mine[k * SUB : (k + 1) * SUB] for k in range(tiles)]
            xs.append(sweep(mine, gs[i], y[i * tall : (i + 1) * tall]))
        for step in range(STEPS - 1):
            flat = jnp.concatenate([z for mine in xs for z in mine], axis=0)
            high = flat.astype(BF16)
            y = dot(jnp.concatenate([high, (flat - high.astype(F32)).astype(BF16)], axis=1), shift[...])
            xs = [sweep(xs[i], gs[i], y[i * tall : (i + 1) * tall]) for i in range(chunk)]
        for i in range(chunk):
            for k in range(tiles):
                done[base + i, k * SUB : (k + 1) * SUB] = xs[i][k]
        pltpu.make_async_copy(done.at[pl.ds(base, chunk)], out.at[pl.ds(base, chunk)], sem).start()
        return 0

    lax.fori_loop(0, count // chunk, one, 0, unroll=count // chunk)
    pltpu.make_async_copy(done, out, sem).wait()


def shift_table():
    table = np.zeros((LANES, 2 * LANES), np.float32)
    for i in range(LANES):
        table[i, i] = -4.0
        for j in (i - 1, i + 1):
            if 0 <= j and j // PC == i // PC:
                table[i, j] = 1.0
        table[i, (i + PC) % LANES] = 1.0
        table[i, LANES + (i + PC) % LANES] = 1.0
    return np.concatenate([table, table], axis=0)


def sweeps(strip, state, ghosts, rate):
    vmem = pl.BlockSpec(memory_space=pltpu.VMEM)
    return pl.pallas_call(
        sweep_kernel,
        in_specs=[pl.BlockSpec(memory_space=pltpu.SMEM)] + [vmem] * 4,
        out_specs=pl.BlockSpec(memory_space=pltpu.HBM),
        out_shape=pltpu.HBM(state.shape, F32),
        scratch_shapes=[pltpu.VMEM(state.shape, F32), pltpu.SemaphoreType.DMA],
        compiler_params=pltpu.CompilerParams(vmem_limit_bytes=24 * MIB),
    )(strip, state, ghosts, rate, jnp.asarray(shift_table(), BF16))


def interp_table():
    coarse = PC // 2
    table = np.zeros((2, coarse, 2, PC), np.float32)
    for side in range(2):
        for c in range(PC):
            near = c // 2
            second = max(near - 1, 0) if c % 2 == 0 else min(near + 1, coarse - 1)
            table[side, near, side, c] += 0.75
            table[side, second, side, c] += 0.25
    return table.reshape(2 * coarse, 2 * PC)


def shards(fields, new_owner, leaflet, stiffness, coarse, coarse_of_slot, viscosity):
    devices = lax.axis_size("axial") * lax.axis_size("azim")
    patch_count = fields.shape[0]
    slots = devices * SLOTS_EACH

    leaf = in_vmem(leaflet)
    row_one, row_two, sides = first_part(leaf)
    side_two = exchange(sides, "azim", 1)
    side_one = exchange(sides, "azim", 0)
    row_two = exchange(row_two, "axial", 1)
    row_one = exchange(row_one, "axial", 0)
    lap, target, coupling, spread = laplace(leaf, new_owner.reshape(1, patch_count), stiffness)
    held = in_vmem(to_tiles(fields))
    image, rest = main_part(target, held, lap, spread, slots)
    sent = edge_part(target, rest, coupling, row_two, row_one, side_two, side_one, image)
    arrived = lax.all_to_all(sent.reshape(devices, -1, LANES), ALL, split_axis=0, concat_axis=0, tiled=True)
    state = arrived.reshape(slots, -1, LANES)

    strips = coarse.shape[0]
    ghosts = jnp.dot(
        coarse.reshape(strips * FIELDS, -1), jnp.asarray(interp_table()), precision=lax.Precision.HIGHEST
    ).reshape(strips, FIELDS, LANES)
    ghosts = jnp.concatenate([ghosts, ghosts], axis=1)
    rate = jnp.broadcast_to(jnp.concatenate([viscosity, viscosity])[:, None], (SUB, LANES))
    return from_tiles(sweeps(coarse_of_slot, state, ghosts, rate))


def solution(mesh):
    placed = (
        P(ALL, None, None),
        P(ALL, None),
        P(None, "axial", "azim"),
        P(),
        P(ALL, None),
        P(ALL),
        P(),
    )
    return jax.shard_map(
        shards,
        mesh=mesh,
        in_specs=placed,
        out_specs=P(ALL, None, None),
        check_vma=False,
    )
```

```python
import jax
import jax.numpy as jnp
import numpy as np
from jax import lax
from jax.experimental import pallas as pl
from jax.experimental.pallas import tpu as pltpu
from jax.sharding import PartitionSpec as P

PC = 64
FIELDS = 4
STEPS = 2
SPREAD = 0.25
LANES = 128
SUB = 8
SLOTS_EACH = 2
ALL = ("axial", "azim")
F32 = jnp.float32
BF16 = jnp.bfloat16
MIB = 2**20


def to_tiles(x):
    n = x.shape[0]
    return x.reshape(n, FIELDS, -1, LANES).transpose(0, 2, 1, 3).reshape(n, -1, LANES)


def from_tiles(x):
    n = x.shape[0]
    return x.reshape(n, -1, FIELDS, LANES).transpose(0, 2, 1, 3).reshape(n, FIELDS, -1)


def iota(shape, dim):
    return lax.broadcasted_iota(jnp.int32, shape, dim)


def dot(a, b):
    return jnp.dot(a, b, preferred_element_type=F32)


def in_hbm(x):
    return pltpu.with_memory_space_constraint(x, pltpu.HBM)


def in_vmem(x):
    return pltpu.with_memory_space_constraint(x, pltpu.VMEM)


def where_one(mask):
    return jnp.where(mask, 1.0, 0.0).astype(BF16)


def sides_kernel(leaf, sides):
    records, rows, cols = leaf.shape
    spot = jnp.where(iota((cols, LANES), 1) // rows % 2 == 0, 0, cols - 1)
    wide = dot(leaf[...].reshape(-1, cols), where_one(iota((cols, LANES), 0) == spot))
    r = iota((records * rows, LANES), 0) % rows
    wide = jnp.where(iota((records * rows, LANES), 1) % rows == r, wide, 0.0).astype(BF16)
    gather = iota((records, records * rows), 1) // rows == iota((records, records * rows), 0)
    sides[...] = dot(where_one(gather), wide).astype(BF16)


def rows_kernel(leaf, one, two):
    records, rows, cols = leaf.shape
    half = rows // 2
    odd = lax.axis_index("axial") % 2
    pick = iota((records, records * half), 1) - iota((records, records * half), 0) * half
    first = dot(where_one(pick == 0), leaf[:, :half].reshape(-1, cols))
    last = dot(where_one(pick == half - 1), leaf[:, half:].reshape(-1, cols))
    one[...] = jnp.where(odd == 0, last, first).astype(BF16)
    two[...] = jnp.where(odd == 0, first, last).astype(BF16)


def edge_call(kernel, leaf, shapes):
    vmem = pl.BlockSpec(memory_space=pltpu.VMEM)
    return pl.pallas_call(
        kernel,
        in_specs=[vmem],
        out_specs=[vmem] * len(shapes),
        out_shape=[pltpu.VMEM(s, BF16) for s in shapes],
        compiler_params=pltpu.CompilerParams(vmem_limit_bytes=16 * MIB),
        cost_estimate=pl.CostEstimate(flops=10**8, bytes_accessed=MIB, transcendentals=0),
    )(leaf)


def laplace_kernel(
    leaf, owner_hbm, stiff_hbm, lap, target, coupling, spread, owner, stiffness, small_sem
):
    small = [
        pltpu.make_async_copy(owner_hbm, owner, small_sem.at[0]),
        pltpu.make_async_copy(stiff_hbm, stiffness, small_sem.at[1]),
    ]
    for c in small:
        c.start()
    records, rows, cols = leaf.shape

    group = 256 // rows
    a, b = iota((group * rows, group * rows), 0), iota((group * rows, group * rows), 1)
    beside = where_one((jnp.abs(a - b) == 1) & (a // rows == b // rows))
    a, b = iota((cols, cols), 0), iota((cols, cols), 1)
    along = jnp.where(a == b, -4.0, jnp.where(jnp.abs(a - b) == 1, 1.0, 0.0)).astype(BF16)
    for g in range(records // group):
        x = leaf[g * group : (g + 1) * group].reshape(group * rows, cols)
        y = (dot(beside, x) + dot(x, along)).reshape(group, rows, cols)
        for n in range(rows // SUB):
            part = y[:, n * SUB : (n + 1) * SUB].reshape(group * SUB, cols)
            lap[n, g * group * SUB : (g + 1) * group * SUB] = part.astype(BF16)
    small[0].wait()
    devices, patches = LANES, owner.shape[1]
    mine = owner[...] == iota((devices, patches), 0)
    before = where_one(iota((patches, patches), 0) < iota((patches, patches), 1))
    earlier = dot(where_one(mine), before)
    ranked = jnp.sum(jnp.where(mine, earlier, 0.0), axis=0, keepdims=True)
    target[...] = owner[...] * SLOTS_EACH + ranked.astype(jnp.int32)

    small[1].wait()
    half = records // 2
    a, b = iota((records, records), 0), iota((records, records), 1)
    old = a % FIELDS * (records // FIELDS) + a % half // FIELDS * 2 + a // half
    ordered = (dot(where_one(b == old), stiffness[...]) * SPREAD).astype(BF16)
    coupling[...] = ordered

    wide = records * SUB
    lift = where_one(iota((records, wide), 1) // SUB == iota((records, wide), 0))
    lifted = dot(ordered, lift)
    within = iota((half, wide), 1) % SUB
    for p in range(2):
        for r in range(SUB):
            part = jnp.where(within == r, lifted[p * half : (p + 1) * half], 0.0)
            at = (p * SUB + r) * half
            spread[at : at + half] = part.astype(BF16)


def laplace(leaf, owner, stiffness):
    records, rows, cols = leaf.shape
    vmem = pl.BlockSpec(memory_space=pltpu.VMEM)
    hbm = pl.BlockSpec(memory_space=pltpu.HBM)
    return pl.pallas_call(
        laplace_kernel,
        in_specs=[vmem, hbm, hbm],
        out_specs=[vmem] * 4,
        out_shape=[
            pltpu.VMEM((rows // SUB, records * SUB, cols), BF16),
            jax.ShapeDtypeStruct(owner.shape, jnp.int32),
            pltpu.VMEM((records, records), BF16),
            pltpu.VMEM((records * SUB, records * SUB), BF16),
        ],
        scratch_shapes=[
            pltpu.VMEM(owner.shape, jnp.int32),
            pltpu.VMEM(stiffness.shape, BF16),
            pltpu.SemaphoreType.DMA((2,)),
        ],
        compiler_params=pltpu.CompilerParams(vmem_limit_bytes=16 * MIB),
        cost_estimate=pl.CostEstimate(flops=5 * 10**8, bytes_accessed=3 * MIB, transcendentals=0),
    )(leaf, in_hbm(owner), in_hbm(stiffness))


def exchange(x, axis, offset):
    size = lax.axis_size(axis)
    pairs = [(i % size, (i + 1) % size) for i in range(offset, size + offset, 2)]
    return lax.ppermute(x, axis, pairs + [(j, i) for i, j in pairs])


def halves(a, b, low, t):
    a, b = a[:, t * LANES : (t + 1) * LANES], b[:, t * LANES : (t + 1) * LANES]
    return jnp.where(low, a, pltpu.roll(b, PC, 1)), jnp.where(low, pltpu.roll(a, PC, 1), b)


def edge_patches(rows, quarters):
    return [
        (r, q) for r in range(rows) for q in range(quarters) if r in (0, rows - 1) or q in (0, quarters - 1)
    ]


def main_kernel(target, fields, lap, spread, image, rest):
    blocks, _, cols = lap.shape
    half = fields.shape[1]
    rows = blocks * SUB
    quarters = cols // PC
    low = iota((half, LANES), 1) < PC
    edge = {rq: i for i, rq in enumerate(edge_patches(rows, quarters))}
    image[...] = jnp.zeros_like(image)
    for n in range(blocks):
        tension = dot(spread[...], lap[n])
        for k in range(SUB):
            r = n * SUB + k
            a = tension[k * half : (k + 1) * half]
            b = tension[(SUB + k) * half : (SUB + k + 1) * half]
            for t in range(cols // LANES):
                for h, sheet in enumerate(halves(a, b, low, t)):
                    q = 2 * t + h
                    patch = r * quarters + q
                    forced = fields[patch] + sheet
                    if (r, q) in edge:
                        rest[edge[r, q]] = forced
                    else:
                        image[target[0, patch]] = forced.astype(BF16)


def main_part(target, fields, lap, spread, slots):
    _, tall, _ = fields.shape
    blocks, _, cols = lap.shape
    vmem = pl.BlockSpec(memory_space=pltpu.VMEM)
    count = len(edge_patches(blocks * SUB, cols // PC))
    return pl.pallas_call(
        main_kernel,
        in_specs=[pl.BlockSpec(memory_space=pltpu.SMEM), vmem, vmem, vmem],
        out_specs=[vmem, vmem],
        out_shape=[pltpu.VMEM((slots, tall, LANES), BF16), pltpu.VMEM((count, tall, LANES), F32)],
        compiler_params=pltpu.CompilerParams(vmem_limit_bytes=16 * MIB),
        cost_estimate=pl.CostEstimate(flops=10**9, bytes_accessed=4 * MIB, transcendentals=0),
    )(target, fields, lap, spread)


def edge_kernel(target, rest, coupling, row_two, row_one, side_two, side_one, image_in, image, sent, sem):
    del image_in
    records, cols = row_one.shape
    half = records // 2
    quarters = cols // PC
    rows = LANES // 4
    low = iota((half, LANES), 1) < PC

    lane = iota((records, LANES), 1)
    odd = lax.axis_index("azim") % 2
    near = jnp.where((lane // rows + odd) % 2 == 0, side_one[...].astype(F32), side_two[...].astype(F32)).astype(BF16)
    both = dot(coupling[...], near)
    both = jnp.where(low, both[:half], both[half:])
    lane = iota((half, LANES), 1)
    column = jnp.concatenate([jnp.where(lane % rows == r, both, 0.0) for r in range(rows)], axis=0)
    high = column.astype(BF16)
    split = jnp.concatenate([high, (column - high.astype(F32)).astype(BF16)], axis=1)
    a, b = iota((2 * LANES, 2 * LANES), 0), iota((2 * LANES, 2 * LANES), 1)
    p, s = a // PC % 2, a // rows % 2
    split = dot(split, where_one(b == jnp.where(s == 1, p * PC, LANES + p * PC + PC - 1)))

    place, size = lax.axis_index("axial"), lax.axis_size("axial")
    odd = place % 2 == 1
    one, two = row_one[...].astype(F32), row_two[...].astype(F32)
    two = jnp.where((place == 0) | (place == size - 1), 0.0, two)
    ends = {}
    for r, row in ((0, jnp.where(odd, one, two)), (rows - 1, jnp.where(odd, two, one))):
        whole = dot(coupling[...], row.astype(BF16))
        for t in range(cols // LANES):
            for h, sheet in enumerate(halves(whole[:half], whole[half:], low, t)):
                ends[r, 2 * t + h] = sheet

    listed = edge_patches(rows, quarters)
    for i, (r, q) in enumerate(listed):
        forced = rest[i]
        if q == 0:
            forced = forced + split[r * half : (r + 1) * half, :LANES]
        if q == quarters - 1:
            forced = forced + split[r * half : (r + 1) * half, LANES:]
        if (r, q) in ends:
            forced = forced + ends[r, q]
        image[target[0, r * quarters + q]] = forced.astype(BF16)
    whole = pltpu.make_async_copy(image, sent, sem)
    whole.start()
    whole.wait()


def edge_part(target, rest, coupling, row_two, row_one, side_two, side_one, image):
    vmem = pl.BlockSpec(memory_space=pltpu.VMEM)
    _, sent = pl.pallas_call(
        edge_kernel,
        in_specs=[pl.BlockSpec(memory_space=pltpu.SMEM)] + [vmem] * 7,
        out_specs=[vmem, pl.BlockSpec(memory_space=pltpu.HBM)],
        out_shape=[pltpu.VMEM(image.shape, BF16), pltpu.HBM(image.shape, BF16)],
        scratch_shapes=[pltpu.SemaphoreType.DMA],
        input_output_aliases={7: 0},
        compiler_params=pltpu.CompilerParams(vmem_limit_bytes=16 * MIB),
        cost_estimate=pl.CostEstimate(flops=2 * 10**8, bytes_accessed=2 * MIB, transcendentals=0),
    )(target, rest, coupling, row_two, row_one, side_two, side_one, image)
    return sent


def sweep_kernel(strip, state, ghosts, rate, shift, out, done, sem):
    count, tall, _ = state.shape
    lane = iota((SUB, LANES), 1)
    row = iota((SUB, LANES), 0)
    first = (lane < PC) & (row < FIELDS)
    last = (lane >= PC) & (row >= FIELDS)
    v = rate[...]
    tiles = tall // SUB
    chunk = 8

    def sweep(x, g, y):
        flat = [y[k * SUB : (k + 1) * SUB, :LANES] for k in range(tiles)]
        across = [y[k * SUB : (k + 1) * SUB, LANES:] for k in range(tiles)]
        ext = [g] + [pltpu.roll(z, FIELDS, 0) for z in across] + [g]
        new = []
        for k in range(tiles):
            vertical = jnp.where(first, ext[k], jnp.where(last, ext[k + 2], ext[k + 1]))
            new.append(x[k] + v * (flat[k] + vertical))
        return new

    def one(c, _):
        base = pl.multiple_of(c * chunk, chunk)
        x = state[pl.ds(base, chunk)].reshape(chunk * tall, LANES)
        y = dot(x, shift[:LANES])
        xs = []
        gs = []
        for i in range(chunk):
            gs.append(ghosts[strip[base + i]])
            mine = x[i * tall : (i + 1) * tall].astype(F32)
            mine = [mine[k * SUB : (k + 1) * SUB] for k in range(tiles)]
            xs.append(sweep(mine, gs[i], y[i * tall : (i + 1) * tall]))
        for step in range(STEPS - 1):
            flat = jnp.concatenate([z for mine in xs for z in mine], axis=0)
            high = flat.astype(BF16)
            y = dot(jnp.concatenate([high, (flat - high.astype(F32)).astype(BF16)], axis=1), shift[...])
            xs = [sweep(xs[i], gs[i], y[i * tall : (i + 1) * tall]) for i in range(chunk)]
        for i in range(chunk):
            for k in range(tiles):
                done[base + i, k * SUB : (k + 1) * SUB] = xs[i][k]
        pltpu.make_async_copy(done.at[pl.ds(base, chunk)], out.at[pl.ds(base, chunk)], sem).start()
        return 0

    lax.fori_loop(0, count // chunk, one, 0, unroll=count // chunk)
    pltpu.make_async_copy(done, out, sem).wait()


def shift_table():
    table = np.zeros((LANES, 2 * LANES), np.float32)
    for i in range(LANES):
        table[i, i] = -4.0
        for j in (i - 1, i + 1):
            if 0 <= j and j // PC == i // PC:
                table[i, j] = 1.0
        table[i, (i + PC) % LANES] = 1.0
        table[i, LANES + (i + PC) % LANES] = 1.0
    return np.concatenate([table, table], axis=0)


def sweeps(strip, state, ghosts, rate):
    vmem = pl.BlockSpec(memory_space=pltpu.VMEM)
    return pl.pallas_call(
        sweep_kernel,
        in_specs=[pl.BlockSpec(memory_space=pltpu.SMEM)] + [vmem] * 4,
        out_specs=pl.BlockSpec(memory_space=pltpu.HBM),
        out_shape=pltpu.HBM(state.shape, F32),
        scratch_shapes=[pltpu.VMEM(state.shape, F32), pltpu.SemaphoreType.DMA],
        compiler_params=pltpu.CompilerParams(vmem_limit_bytes=24 * MIB),
    )(strip, state, ghosts, rate, jnp.asarray(shift_table(), BF16))


def interp_table():
    coarse = PC // 2
    table = np.zeros((2, coarse, 2, PC), np.float32)
    for side in range(2):
        for c in range(PC):
            near = c // 2
            second = max(near - 1, 0) if c % 2 == 0 else min(near + 1, coarse - 1)
            table[side, near, side, c] += 0.75
            table[side, second, side, c] += 0.25
    return table.reshape(2 * coarse, 2 * PC)


def shards(fields, new_owner, leaflet, stiffness, coarse, coarse_of_slot, viscosity):
    devices = lax.axis_size("axial") * lax.axis_size("azim")
    patch_count = fields.shape[0]
    slots = devices * SLOTS_EACH

    leaf = in_vmem(leaflet)
    records, _, cols = leaf.shape
    (sides,) = edge_call(sides_kernel, leaf, [(records, LANES)])
    sides, leaf = lax.optimization_barrier((sides, leaf))
    row_one, row_two = edge_call(rows_kernel, leaf, [(records, cols)] * 2)
    side_two = exchange(sides, "azim", 1)
    side_one = exchange(sides, "azim", 0)
    row_two = exchange(row_two, "axial", 1)
    row_one = exchange(row_one, "axial", 0)
    lap, target, coupling, spread = laplace(leaf, new_owner.reshape(1, patch_count), stiffness)
    held = in_vmem(to_tiles(fields))
    image, rest = main_part(target, held, lap, spread, slots)
    sent = edge_part(target, rest, coupling, row_two, row_one, side_two, side_one, image)
    arrived = lax.all_to_all(sent.reshape(devices, -1, LANES), ALL, split_axis=0, concat_axis=0, tiled=True)
    state = arrived.reshape(slots, -1, LANES)

    strips = coarse.shape[0]
    ghosts = jnp.dot(
        coarse.reshape(strips * FIELDS, -1), jnp.asarray(interp_table()), precision=lax.Precision.HIGHEST
    ).reshape(strips, FIELDS, LANES)
    ghosts = jnp.concatenate([ghosts, ghosts], axis=1)
    rate = jnp.broadcast_to(jnp.concatenate([viscosity, viscosity])[:, None], (SUB, LANES))
    return from_tiles(sweeps(coarse_of_slot, state, ghosts, rate))


def solution(mesh):
    placed = (
        P(ALL, None, None),
        P(ALL, None),
        P(None, "axial", "azim"),
        P(),
        P(ALL, None),
        P(ALL),
        P(),
    )
    return jax.shard_map(
        shards,
        mesh=mesh,
        in_specs=placed,
        out_specs=P(ALL, None, None),
        check_vma=False,
    )
```

```python
import jax
import jax.numpy as jnp
import numpy as np
from jax import lax
from jax.experimental import pallas as pl
from jax.experimental.pallas import tpu as pltpu
from jax.sharding import PartitionSpec as P

PC = 64
FIELDS = 4
STEPS = 2
SPREAD = 0.25
LANES = 128
SUB = 8
SLOTS_EACH = 2
ALL = ("axial", "azim")
F32 = jnp.float32
BF16 = jnp.bfloat16
MIB = 2**20


def to_tiles(x):
    n = x.shape[0]
    return x.reshape(n, FIELDS, -1, LANES).transpose(0, 2, 1, 3).reshape(n, -1, LANES)


def from_tiles(x):
    n = x.shape[0]
    return x.reshape(n, -1, FIELDS, LANES).transpose(0, 2, 1, 3).reshape(n, FIELDS, -1)


def iota(shape, dim):
    return lax.broadcasted_iota(jnp.int32, shape, dim)


def dot(a, b):
    return jnp.dot(a, b, preferred_element_type=F32)


def in_hbm(x):
    return pltpu.with_memory_space_constraint(x, pltpu.HBM)


def in_vmem(x):
    return pltpu.with_memory_space_constraint(x, pltpu.VMEM)


def where_one(mask):
    return jnp.where(mask, 1.0, 0.0).astype(BF16)


def first_kernel(leaf, one, two, sides):
    records, rows, cols = leaf.shape
    half = rows // 2
    odd = lax.axis_index("axial") % 2
    spot = jnp.where(iota((cols, LANES), 1) // rows % 2 == 0, 0, cols - 1)
    wide = dot(leaf[...].reshape(-1, cols), where_one(iota((cols, LANES), 0) == spot))
    r = iota((records * rows, LANES), 0) % rows
    wide = jnp.where(iota((records * rows, LANES), 1) % rows == r, wide, 0.0).astype(BF16)
    gather = iota((records, records * rows), 1) // rows == iota((records, records * rows), 0)
    sides[...] = dot(where_one(gather), wide).astype(BF16)
    pick = iota((records, records * half), 1) - iota((records, records * half), 0) * half
    first = dot(where_one(pick == 0), leaf[:, :half].reshape(-1, cols))
    last = dot(where_one(pick == half - 1), leaf[:, half:].reshape(-1, cols))
    one[...] = jnp.where(odd == 0, last, first).astype(BF16)
    two[...] = jnp.where(odd == 0, first, last).astype(BF16)


def first_part(leaf):
    records, rows, cols = leaf.shape
    vmem = pl.BlockSpec(memory_space=pltpu.VMEM)
    shapes = [(records, cols), (records, cols), (records, LANES)]
    return pl.pallas_call(
        first_kernel,
        in_specs=[vmem],
        out_specs=[vmem] * 3,
        out_shape=[pltpu.VMEM(s, BF16) for s in shapes],
        compiler_params=pltpu.CompilerParams(vmem_limit_bytes=16 * MIB),
        cost_estimate=pl.CostEstimate(flops=10**8, bytes_accessed=MIB, transcendentals=0),
    )(leaf)


def laplace_kernel(
    leaf, owner_hbm, stiff_hbm, lap, target, coupling, spread, owner, stiffness, small_sem
):
    small = [
        pltpu.make_async_copy(owner_hbm, owner, small_sem.at[0]),
        pltpu.make_async_copy(stiff_hbm, stiffness, small_sem.at[1]),
    ]
    for c in small:
        c.start()
    records, rows, cols = leaf.shape

    group = 256 // rows
    a, b = iota((group * rows, group * rows), 0), iota((group * rows, group * rows), 1)
    beside = where_one((jnp.abs(a - b) == 1) & (a // rows == b // rows))
    a, b = iota((cols, cols), 0), iota((cols, cols), 1)
    along = jnp.where(a == b, -4.0, jnp.where(jnp.abs(a - b) == 1, 1.0, 0.0)).astype(BF16)
    for g in range(records // group):
        x = leaf[g * group : (g + 1) * group].reshape(group * rows, cols)
        y = (dot(beside, x) + dot(x, along)).reshape(group, rows, cols)
        for n in range(rows // SUB):
            part = y[:, n * SUB : (n + 1) * SUB].reshape(group * SUB, cols)
            lap[n, g * group * SUB : (g + 1) * group * SUB] = part.astype(BF16)
    small[0].wait()
    devices, patches = LANES, owner.shape[1]
    mine = owner[...] == iota((devices, patches), 0)
    before = where_one(iota((patches, patches), 0) < iota((patches, patches), 1))
    earlier = dot(where_one(mine), before)
    ranked = jnp.sum(jnp.where(mine, earlier, 0.0), axis=0, keepdims=True)
    target[...] = owner[...] * SLOTS_EACH + ranked.astype(jnp.int32)

    small[1].wait()
    half = records // 2
    a, b = iota((records, records), 0), iota((records, records), 1)
    old = a % FIELDS * (records // FIELDS) + a % half // FIELDS * 2 + a // half
    ordered = (dot(where_one(b == old), stiffness[...]) * SPREAD).astype(BF16)
    coupling[...] = ordered

    wide = records * SUB
    lift = where_one(iota((records, wide), 1) // SUB == iota((records, wide), 0))
    lifted = dot(ordered, lift)
    within = iota((half, wide), 1) % SUB
    for p in range(2):
        for r in range(SUB):
            part = jnp.where(within == r, lifted[p * half : (p + 1) * half], 0.0)
            at = (p * SUB + r) * half
            spread[at : at + half] = part.astype(BF16)


def laplace(leaf, owner, stiffness):
    records, rows, cols = leaf.shape
    vmem = pl.BlockSpec(memory_space=pltpu.VMEM)
    hbm = pl.BlockSpec(memory_space=pltpu.HBM)
    return pl.pallas_call(
        laplace_kernel,
        in_specs=[vmem, hbm, hbm],
        out_specs=[vmem] * 4,
        out_shape=[
            pltpu.VMEM((rows // SUB, records * SUB, cols), BF16),
            jax.ShapeDtypeStruct(owner.shape, jnp.int32),
            pltpu.VMEM((records, records), BF16),
            pltpu.VMEM((records * SUB, records * SUB), BF16),
        ],
        scratch_shapes=[
            pltpu.VMEM(owner.shape, jnp.int32),
            pltpu.VMEM(stiffness.shape, BF16),
            pltpu.SemaphoreType.DMA((2,)),
        ],
        compiler_params=pltpu.CompilerParams(vmem_limit_bytes=16 * MIB),
        cost_estimate=pl.CostEstimate(flops=5 * 10**8, bytes_accessed=3 * MIB, transcendentals=0),
    )(leaf, in_hbm(owner), in_hbm(stiffness))


def exchange(x, axis, offset):
    size = lax.axis_size(axis)
    pairs = [(i % size, (i + 1) % size) for i in range(offset, size + offset, 2)]
    return lax.ppermute(x, axis, pairs + [(j, i) for i, j in pairs])


def halves(a, b, low, t):
    a, b = a[:, t * LANES : (t + 1) * LANES], b[:, t * LANES : (t + 1) * LANES]
    return jnp.where(low, a, pltpu.roll(b, PC, 1)), jnp.where(low, pltpu.roll(a, PC, 1), b)


def edge_patches(rows, quarters):
    return [
        (r, q) for r in range(rows) for q in range(quarters) if r in (0, rows - 1) or q in (0, quarters - 1)
    ]


def main_kernel(target, fields, lap, spread, image, rest):
    blocks, _, cols = lap.shape
    half = fields.shape[1]
    rows = blocks * SUB
    quarters = cols // PC
    low = iota((half, LANES), 1) < PC
    edge = {rq: i for i, rq in enumerate(edge_patches(rows, quarters))}
    image[...] = jnp.zeros_like(image)
    for n in range(blocks):
        tension = dot(spread[...], lap[n])
        for k in range(SUB):
            r = n * SUB + k
            a = tension[k * half : (k + 1) * half]
            b = tension[(SUB + k) * half : (SUB + k + 1) * half]
            for t in range(cols // LANES):
                for h, sheet in enumerate(halves(a, b, low, t)):
                    q = 2 * t + h
                    patch = r * quarters + q
                    forced = fields[patch] + sheet
                    if (r, q) in edge:
                        rest[edge[r, q]] = forced
                    else:
                        image[target[0, patch]] = forced.astype(BF16)


def main_part(target, fields, lap, spread, slots):
    _, tall, _ = fields.shape
    blocks, _, cols = lap.shape
    vmem = pl.BlockSpec(memory_space=pltpu.VMEM)
    count = len(edge_patches(blocks * SUB, cols // PC))
    return pl.pallas_call(
        main_kernel,
        in_specs=[pl.BlockSpec(memory_space=pltpu.SMEM), vmem, vmem, vmem],
        out_specs=[vmem, vmem],
        out_shape=[pltpu.VMEM((slots, tall, LANES), BF16), pltpu.VMEM((count, tall, LANES), F32)],
        compiler_params=pltpu.CompilerParams(vmem_limit_bytes=16 * MIB),
        cost_estimate=pl.CostEstimate(flops=10**9, bytes_accessed=4 * MIB, transcendentals=0),
    )(target, fields, lap, spread)


def edge_kernel(target, rest, coupling, row_two, row_one, side_two, side_one, image_in, image, sent, sem):
    del image_in
    records, cols = row_one.shape
    half = records // 2
    quarters = cols // PC
    rows = LANES // 4
    low = iota((half, LANES), 1) < PC

    lane = iota((records, LANES), 1)
    odd = lax.axis_index("azim") % 2
    near = jnp.where((lane // rows + odd) % 2 == 0, side_one[...].astype(F32), side_two[...].astype(F32)).astype(BF16)
    both = dot(coupling[...], near)
    both = jnp.where(low, both[:half], both[half:])
    lane = iota((half, LANES), 1)
    column = jnp.concatenate([jnp.where(lane % rows == r, both, 0.0) for r in range(rows)], axis=0)
    high = column.astype(BF16)
    split = jnp.concatenate([high, (column - high.astype(F32)).astype(BF16)], axis=1)
    a, b = iota((2 * LANES, 2 * LANES), 0), iota((2 * LANES, 2 * LANES), 1)
    p, s = a // PC % 2, a // rows % 2
    split = dot(split, where_one(b == jnp.where(s == 1, p * PC, LANES + p * PC + PC - 1)))

    place, size = lax.axis_index("axial"), lax.axis_size("axial")
    odd = place % 2 == 1
    one, two = row_one[...].astype(F32), row_two[...].astype(F32)
    two = jnp.where((place == 0) | (place == size - 1), 0.0, two)
    ends = {}
    for r, row in ((0, jnp.where(odd, one, two)), (rows - 1, jnp.where(odd, two, one))):
        whole = dot(coupling[...], row.astype(BF16))
        for t in range(cols // LANES):
            for h, sheet in enumerate(halves(whole[:half], whole[half:], low, t)):
                ends[r, 2 * t + h] = sheet

    listed = edge_patches(rows, quarters)
    for i, (r, q) in enumerate(listed):
        forced = rest[i]
        if q == 0:
            forced = forced + split[r * half : (r + 1) * half, :LANES]
        if q == quarters - 1:
            forced = forced + split[r * half : (r + 1) * half, LANES:]
        if (r, q) in ends:
            forced = forced + ends[r, q]
        image[target[0, r * quarters + q]] = forced.astype(BF16)
    whole = pltpu.make_async_copy(image, sent, sem)
    whole.start()
    whole.wait()


def edge_part(target, rest, coupling, row_two, row_one, side_two, side_one, image):
    vmem = pl.BlockSpec(memory_space=pltpu.VMEM)
    _, sent = pl.pallas_call(
        edge_kernel,
        in_specs=[pl.BlockSpec(memory_space=pltpu.SMEM)] + [vmem] * 7,
        out_specs=[vmem, pl.BlockSpec(memory_space=pltpu.HBM)],
        out_shape=[pltpu.VMEM(image.shape, BF16), pltpu.HBM(image.shape, BF16)],
        scratch_shapes=[pltpu.SemaphoreType.DMA],
        input_output_aliases={7: 0},
        compiler_params=pltpu.CompilerParams(vmem_limit_bytes=16 * MIB),
        cost_estimate=pl.CostEstimate(flops=2 * 10**8, bytes_accessed=2 * MIB, transcendentals=0),
    )(target, rest, coupling, row_two, row_one, side_two, side_one, image)
    return sent


def sweep_kernel(strip, state, ghosts, rate, shift, out, done, sem):
    count, tall, _ = state.shape
    lane = iota((SUB, LANES), 1)
    row = iota((SUB, LANES), 0)
    first = (lane < PC) & (row < FIELDS)
    last = (lane >= PC) & (row >= FIELDS)
    v = rate[...]
    tiles = tall // SUB
    chunk = 8

    def sweep(x, g, y):
        flat = [y[k * SUB : (k + 1) * SUB, :LANES] for k in range(tiles)]
        across = [y[k * SUB : (k + 1) * SUB, LANES:] for k in range(tiles)]
        ext = [g] + [pltpu.roll(z, FIELDS, 0) for z in across] + [g]
        new = []
        for k in range(tiles):
            vertical = jnp.where(first, ext[k], jnp.where(last, ext[k + 2], ext[k + 1]))
            new.append(x[k] + v * (flat[k] + vertical))
        return new

    def one(c, _):
        base = pl.multiple_of(c * chunk, chunk)
        x = state[pl.ds(base, chunk)].reshape(chunk * tall, LANES)
        y = dot(x, shift[:LANES])
        xs = []
        gs = []
        for i in range(chunk):
            gs.append(ghosts[strip[base + i]])
            mine = x[i * tall : (i + 1) * tall].astype(F32)
            mine = [mine[k * SUB : (k + 1) * SUB] for k in range(tiles)]
            xs.append(sweep(mine, gs[i], y[i * tall : (i + 1) * tall]))
        for step in range(STEPS - 1):
            flat = jnp.concatenate([z for mine in xs for z in mine], axis=0)
            y = dot(flat.astype(BF16), shift[:LANES])
            xs = [sweep(xs[i], gs[i], y[i * tall : (i + 1) * tall]) for i in range(chunk)]
        for i in range(chunk):
            for k in range(tiles):
                done[base + i, k * SUB : (k + 1) * SUB] = xs[i][k]
        pltpu.make_async_copy(done.at[pl.ds(base, chunk)], out.at[pl.ds(base, chunk)], sem).start()
        return 0

    lax.fori_loop(0, count // chunk, one, 0, unroll=count // chunk)
    pltpu.make_async_copy(done, out, sem).wait()


def shift_table():
    table = np.zeros((LANES, 2 * LANES), np.float32)
    for i in range(LANES):
        table[i, i] = -4.0
        for j in (i - 1, i + 1):
            if 0 <= j and j // PC == i // PC:
                table[i, j] = 1.0
        table[i, (i + PC) % LANES] = 1.0
        table[i, LANES + (i + PC) % LANES] = 1.0
    return np.concatenate([table, table], axis=0)


def sweeps(strip, state, ghosts, rate):
    vmem = pl.BlockSpec(memory_space=pltpu.VMEM)
    return pl.pallas_call(
        sweep_kernel,
        in_specs=[pl.BlockSpec(memory_space=pltpu.SMEM)] + [vmem] * 4,
        out_specs=pl.BlockSpec(memory_space=pltpu.HBM),
        out_shape=pltpu.HBM(state.shape, F32),
        scratch_shapes=[pltpu.VMEM(state.shape, F32), pltpu.SemaphoreType.DMA],
        compiler_params=pltpu.CompilerParams(vmem_limit_bytes=24 * MIB),
    )(strip, state, ghosts, rate, jnp.asarray(shift_table(), BF16))


def interp_table():
    coarse = PC // 2
    table = np.zeros((2, coarse, 2, PC), np.float32)
    for side in range(2):
        for c in range(PC):
            near = c // 2
            second = max(near - 1, 0) if c % 2 == 0 else min(near + 1, coarse - 1)
            table[side, near, side, c] += 0.75
            table[side, second, side, c] += 0.25
    return table.reshape(2 * coarse, 2 * PC)


def shards(fields, new_owner, leaflet, stiffness, coarse, coarse_of_slot, viscosity):
    devices = lax.axis_size("axial") * lax.axis_size("azim")
    patch_count = fields.shape[0]
    slots = devices * SLOTS_EACH

    leaf = in_vmem(leaflet)
    row_one, row_two, sides = first_part(leaf)
    side_two = exchange(sides, "azim", 1)
    side_one = exchange(sides, "azim", 0)
    row_two = exchange(row_two, "axial", 1)
    row_one = exchange(row_one, "axial", 0)
    lap, target, coupling, spread = laplace(leaf, new_owner.reshape(1, patch_count), stiffness)
    held = in_vmem(to_tiles(fields))
    image, rest = main_part(target, held, lap, spread, slots)
    sent = edge_part(target, rest, coupling, row_two, row_one, side_two, side_one, image)
    arrived = lax.all_to_all(sent.reshape(devices, -1, LANES), ALL, split_axis=0, concat_axis=0, tiled=True)
    state = arrived.reshape(slots, -1, LANES)

    strips = coarse.shape[0]
    ghosts = jnp.dot(
        coarse.reshape(strips * FIELDS, -1), jnp.asarray(interp_table()), precision=lax.Precision.HIGHEST
    ).reshape(strips, FIELDS, LANES)
    ghosts = jnp.concatenate([ghosts, ghosts], axis=1)
    rate = jnp.broadcast_to(jnp.concatenate([viscosity, viscosity])[:, None], (SUB, LANES))
    return from_tiles(sweeps(coarse_of_slot, state, ghosts, rate))


def solution(mesh):
    placed = (
        P(ALL, None, None),
        P(ALL, None),
        P(None, "axial", "azim"),
        P(),
        P(ALL, None),
        P(ALL),
        P(),
    )
    return jax.shard_map(
        shards,
        mesh=mesh,
        in_specs=placed,
        out_specs=P(ALL, None, None),
        check_vma=False,
    )
```
